32 devices in a mesh: groups: 2 (over x), seq: 16 (over z, y, core).
Axes of the slice: x: 2, y: 2, z: 4, core: 2. Of those that a mesh axis runs over, the one named last changes fastest.
Arguments:
- tokens: bfloat16 [8192, 256], P(('groups', 'seq')), parts along dimension 0, may hold values from -6 to 6
- norm_gain: float32 [256], replicated, may hold values from 0.1 to 1.9
- w_in: bfloat16 [256, 768], replicated, may hold values from -0.375 to 0.375
- short_filter: float32 [3, 768], replicated, may hold values from -0.8 to 0.8
- long_filter: float32 [4096, 256], P('seq'), may hold values from -0.09375 to 0.09375
- medium_filter: float32 [128, 256], replicated, may hold values from -0.5 to 0.5
- skip_gain: float32 [256], replicated, may hold values from -1 to 1
- w_out: bfloat16 [256, 256], replicated, may hold values from -0.375 to 0.375
Outputs:
- result: bfloat16 [8192, 256], P(('groups', 'seq')), parts along dimension 0
The draws below stay inside these ranges and needn't reach their ends.
There are 2 independent parts, one for each index of `groups`. The reference program is written for one: setup_inputs(seed, part) draws one part's arguments, and reference() takes and returns one part's arrays. A program takes and returns all parts, laid end to end along the dimension named above; an argument that names none is the same for every part. Nothing has to cross between parts.
All inputs are finite; a program needn't handle non-finite values.
Results may differ from the reference program's by a relative error of at most 0.015.
Values may be sent and summed in bfloat16 or wider, within the bound.
A program may use at most 64 MiB of HBM per device.

```python
import jax
import jax.numpy as jnp
from jax import lax

D = 256
TAPS = 3
MED = 128
TOKENS = 4096


def block_levels(own_key, shape, cuts, low, largest):
    def one(position, parts):
        heights = jax.random.uniform(jax.random.fold_in(jax.random.fold_in(own_key, 6), position), (parts,), jnp.float32, low / len(cuts), largest / len(cuts))
        return jnp.repeat(jnp.exp(heights), shape[position] // parts).reshape((-1,) + (1,) * (len(shape) - position - 1))

    gain = one(*cuts[0])
    for cut in cuts[1:]:
        gain = gain * one(*cut)
    return gain


def bell_draw(key, shape, scale, bound, pieces=(), held_as=jnp.bfloat16):
    array = scale * jax.random.normal(key, shape, jnp.float32)
    if pieces:
        array = array * block_levels(key, shape, pieces, -0.22, 0.18)
    return jnp.clip(array, -bound, bound).astype(held_as)


def setup_inputs(seed: int = 0, part: int = 0) -> dict:
    streams_of = jax.random.split(jax.random.key(seed), 9)
    own_keys = jax.random.split(jax.random.fold_in(streams_of[8], part), 9)
    tokens = bell_draw(own_keys[0], (TOKENS, D), 1.0, 6.0, ((0, 16),))
    norm_gain = jnp.clip(1.0 + 0.18 * jax.random.normal(streams_of[1], (D,), jnp.float32), 0.1, 1.9)
    w_in = bell_draw(streams_of[2], (D, 3 * D), D ** -0.5, 0.375)
    short_filter = jnp.clip(jax.random.uniform(streams_of[3], (TAPS, 3 * D), jnp.float32, -0.8, 0.8), -0.8, 0.8)
    long_filter = bell_draw(streams_of[4], (TOKENS, D), TOKENS ** -0.5, 0.09375, ((0, 16),), jnp.float32)
    medium_filter = bell_draw(streams_of[5], (MED, D), MED ** -0.5, 0.5, (), jnp.float32)
    skip_gain = jnp.clip(jax.random.uniform(streams_of[6], (D,), jnp.float32, -1.0, 1.0), -1.0, 1.0)
    w_out = bell_draw(streams_of[7], (D, D), D ** -0.5, 0.375)
    return {"tokens": tokens, "norm_gain": norm_gain, "w_in": w_in, "short_filter": short_filter, "long_filter": long_filter, "medium_filter": medium_filter, "skip_gain": skip_gain, "w_out": w_out}


epsilon = 1e-06

def reference(tokens, norm_gain, w_in, short_filter, long_filter, medium_filter, skip_gain, w_out):
    inputs = tokens.astype(jnp.float32)
    mean_sq = lax.optimization_barrier(jnp.mean(inputs * inputs, axis=-1, keepdims=True))
    normed = (inputs * lax.rsqrt(mean_sq + epsilon) * norm_gain).astype(jnp.bfloat16)
    projected = jnp.dot(normed, w_in, preferred_element_type=jnp.float32).astype(jnp.bfloat16)
    projected = lax.optimization_barrier(projected).astype(jnp.float32)
    taps_count = short_filter.shape[0]
    padded = jnp.pad(projected, ((taps_count - 1, 0), (0, 0)))
    short_mix = jnp.zeros_like(projected)
    for tap_num in range(taps_count):
        begin = taps_count - 1 - tap_num
        short_mix = short_mix + short_filter[tap_num] * padded[begin:begin + TOKENS]
    query_part = short_mix[:, 0:D]
    key_part = short_mix[:, D:2 * D]
    value_part = short_mix[:, 2 * D:3 * D]
    signal = key_part * value_part
    fft_len = 2 * TOKENS
    spectrum = jnp.fft.rfft(signal, n=fft_len, axis=0) * jnp.fft.rfft(long_filter, n=fft_len, axis=0)
    conv_out = jnp.fft.irfft(spectrum, n=fft_len, axis=0)[:TOKENS].astype(signal.dtype)
    med_pad = jnp.pad(signal, ((MED - 1, 0), (0, 0)))

    def add_tap(tap_num, acc):
        weights = lax.dynamic_slice_in_dim(medium_filter, tap_num, 1, 0)
        window = lax.dynamic_slice_in_dim(med_pad, (MED - 1 - tap_num).astype(jnp.int32), TOKENS, 0)
        return acc + weights * window
    med_out = lax.fori_loop(0, MED, add_tap, jnp.zeros_like(signal))
    mixed_out = (query_part * (conv_out + med_out + skip_gain * signal)).astype(jnp.bfloat16)
    return jnp.dot(mixed_out, w_out, preferred_element_type=jnp.float32).astype(jnp.bfloat16)
```

```python
import functools
import math

import jax
import jax.numpy as jnp
import numpy as np
from jax import lax
from jax.experimental import pallas as pl
from jax.experimental.pallas import tpu as pltpu
from jax.sharding import PartitionSpec as P

epsilon = 1e-06
bf16 = jnp.bfloat16
f32 = jnp.float32


def tables(devices, tok_rows, chans):
    full = devices * tok_rows
    idx = np.arange(devices)
    angle = 2.0 * math.pi * ((idx[:, None] * (4 * idx[None, :] + 1)) % (4 * devices)) / (4 * devices)
    eye = np.eye(chans)
    outer_cos = np.kron(np.cos(angle), eye)
    outer_sin = np.kron(np.sin(angle), eye)
    first = np.concatenate([outer_cos.T, -outer_sin.T], axis=0)
    last = np.concatenate([outer_cos, -outer_sin], axis=1) / full
    pos = np.arange(tok_rows)
    turn = 2.0 * math.pi * ((4 * idx[:, None] + 1) * pos[None, :]) / (4 * full)
    tw_cos = np.repeat(np.cos(turn), chans, axis=0)
    tw_sin = np.repeat(np.sin(turn), chans, axis=0)
    inner = 2.0 * math.pi * (pos[:, None] * pos[None, :] % tok_rows) / tok_rows
    cos_t, sin_t = np.cos(inner), np.sin(inner)
    middle = np.block([[cos_t, -sin_t], [sin_t, cos_t]])
    return (
        first.astype(bf16),
        middle.astype(bf16),
        last.astype(bf16),
        tw_cos.astype(np.float32),
        tw_sin.astype(np.float32),
    )


def dot(a, b):
    return jnp.dot(a, b, preferred_element_type=f32)


def forward(rows, first, middle, tw_cos, tw_sin):
    half = rows.shape[0]
    part = dot(first, rows)
    re, im = part[:half], part[half:]
    turned = jnp.concatenate([re * tw_cos + im * tw_sin, im * tw_cos - re * tw_sin], axis=1)
    return dot(turned.astype(bf16), middle)


def convolve(sig, fil, first, middle, last, tw_cos, tw_sin):
    width = sig.shape[1]
    spec = forward(sig, first, middle, tw_cos, tw_sin)
    gain = forward(fil, first, middle, tw_cos, tw_sin)
    sr, si, gr, gi = spec[:, :width], spec[:, width:], gain[:, :width], gain[:, width:]
    prod = jnp.concatenate([sr * gi + si * gr, sr * gr - si * gi], axis=1).astype(bf16)
    back = dot(prod, middle)
    im, re = back[:, :width], back[:, width:]
    turned = jnp.concatenate([re * tw_cos - im * tw_sin, re * tw_sin + im * tw_cos], axis=0)
    return dot(last, turned.astype(bf16))


def from_behind(array, axis, by):
    devices = lax.axis_size(axis)
    pairs = [(i, i + by) for i in range(devices) if 0 <= i + by < devices]
    return lax.ppermute(array, axis, pairs)


def local(tokens, norm_gain, w_in, short_filter, long_filter, medium_filter, skip_gain, w_out):
    tok_rows, chan_width = tokens.shape
    devices = lax.axis_size("seq")
    my_index = lax.axis_index("seq")
    chans = chan_width // devices
    consts = [jnp.asarray(t) for t in tables(devices, tok_rows, chans)]
    med = jnp.pad(medium_filter, ((0, tok_rows - medium_filter.shape[0]), (0, 0)))
    med = med.at[0].add(skip_gain)
    taps = (long_filter + jnp.where(my_index == 0, med, 0.0)).astype(bf16)
    inputs = tokens.astype(f32)
    mean_sq = jnp.mean(inputs * inputs, axis=-1, keepdims=True)
    normed = (inputs * lax.rsqrt(mean_sq + epsilon) * norm_gain).astype(bf16)
    projected = dot(normed, w_in).astype(bf16)
    taps_count = short_filter.shape[0]
    rim_rows = from_behind(projected[tok_rows - (taps_count - 1) :], "seq", 1)
    extended = jnp.concatenate([rim_rows, projected], axis=0)
    short_mix = jnp.zeros((tok_rows, projected.shape[1]), f32)
    for tap_num in range(taps_count):
        begin = taps_count - 1 - tap_num
        short_mix = short_mix + short_filter[tap_num] * extended[begin : begin + tok_rows]
    query_part = short_mix[:, 0:chan_width]
    signal = short_mix[:, chan_width : 2 * chan_width] * short_mix[:, 2 * chan_width :]

    def spread(array):
        split = array.astype(bf16).T.reshape(devices, chans, tok_rows)
        return lax.all_to_all(split, "seq", 0, 0, tiled=True).reshape(chan_width, tok_rows)

    mixed = convolve(spread(signal), spread(taps), *consts)
    back = spread_back(mixed, devices, chans)
    mixed_out = (query_part * back.T.astype(f32)).astype(bf16)
    return dot(mixed_out, w_out).astype(bf16)


def spread_back(mixed, devices, chans):
    split = mixed.astype(bf16).reshape(devices, chans, mixed.shape[1])
    return lax.all_to_all(split, "seq", 0, 0, tiled=True).reshape(mixed.shape)


def rms_normed(rows, gain):
    rows = rows.astype(f32)
    mean_sq = jnp.mean(rows * rows, axis=-1, keepdims=True)
    return (rows * lax.rsqrt(mean_sq + epsilon) * gain).astype(bf16)


def relative(own, count):
    steps = []
    bit = 1
    while bit < count:
        steps.append((bit, bit * (1 - 2 * (own // bit % 2))))
        bit *= 2
    return [own + sum(step for bit, step in steps if off // bit % 2) for off in range(count - 1, -1, -1)]


def kernel(
    devices,
    tokens_hbm,
    gain_hbm,
    w_in_hbm,
    short_hbm,
    long_hbm,
    med_hbm,
    skip_hbm,
    w_out_hbm,
    all_first_hbm,
    all_turns_hbm,
    all_last_hbm,
    front_first_hbm,
    front_turns_hbm,
    front_last_hbm,
    middle_hbm,
    out_ref,
    tokens,
    gain_ref,
    w_in,
    short_ref,
    long_taps,
    med,
    skip_ref,
    w_out,
    all_first,
    all_turns,
    all_last,
    front_first,
    front_turns,
    front_last,
    middle,
    halo,
    extended,
    signal,
    sends,
    from_front,
    from_back,
    front_out,
    back_out,
    results,
    local_sem,
    halo_sem,
    send_sem,
    recv_sem,
):
    me = lax.axis_index("seq")
    rows, width = tokens.shape
    side = devices // 2
    chans = width // devices
    half = width // 2
    in_front = me < side
    own = lax.rem(me, side)
    cross = relative(own, side)
    same = cross[:-1]
    rim = halo.shape[0]
    barrier = pltpu.get_barrier_semaphore()
    for off in range(1, devices):
        pl.semaphore_signal(
            barrier,
            inc=1,
            device_id={"seq": lax.rem(me + off, devices)},
            device_id_type=pl.DeviceIdType.MESH,
        )
    loads = [
        pltpu.make_async_copy(source, target, local_sem.at[num])
        for num, (source, target) in enumerate(
            [
                (tokens_hbm, tokens),
                (gain_hbm, gain_ref),
                (w_in_hbm, w_in),
                (short_hbm, short_ref),
                (long_hbm, long_taps),
                (med_hbm, med),
                (skip_hbm, skip_ref),
                (middle_hbm, middle),
                (front_first_hbm, front_first),
                (front_turns_hbm, front_turns),
                (front_last_hbm, front_last),
                (all_first_hbm, all_first),
                (all_turns_hbm, all_turns),
                (all_last_hbm, all_last),
                (w_out_hbm, w_out),
            ]
        )
    ]
    for load in loads:
        load.start()

    def remote(source, target, peer, sent, received):
        return pltpu.make_async_remote_copy(
            src_ref=source,
            dst_ref=target,
            send_sem=send_sem.at[sent],
            recv_sem=recv_sem.at[received],
            device_id={"seq": peer},
            device_id_type=pl.DeviceIdType.MESH,
        )

    def received(ref, num):
        remote(ref, ref, 0, num, num).wait_recv()

    def sent(ref, num):
        remote(ref, ref, 0, num, num).wait_send()

    def scatter(kind):
        source, front, back = sends.at[kind], from_front.at[kind], from_back.at[kind]
        near, far = 2 * kind, 2 * kind + 1

        @pl.when(in_front)
        def _():
            for d in cross:
                remote(source.at[1, d], front.at[own, 1], side + d, far, near).start()
            for d in same:
                remote(source.at[:, d], front.at[own], d, near, near).start()
            front[own] = source[:, own]

        @pl.when(jnp.logical_not(in_front))
        def _():
            for d in cross:
                remote(source.at[0, d], back.at[own], d, near, far).start()
            for d in same:
                remote(source.at[1, d], back.at[own], side + d, far, far).start()
            back[own] = source[1, own]

    def project(part_normed, begin):
        return dot(part_normed, w_in[:, begin:]).astype(bf16).astype(f32)

    def mix(part, begin, count):
        cols = pl.ds(part * width, width)
        total = short_ref[0:1, cols] * extended[rim + begin : rim + begin + count, cols]
        for tap in range(1, short_ref.shape[0]):
            start = rim + begin - tap
            total = total + short_ref[tap : tap + 1, cols] * extended[start : start + count, cols]
        return total

    def turn_signal(begin, count):
        block = signal[begin : begin + count, :].T.astype(bf16)
        sends[1, :, :, :, begin : begin + count] = block.reshape(2, side, chans, count)

    for load in loads[:3]:
        load.wait()
    normed = rms_normed(tokens[...], gain_ref[...])
    extended[rim:, width:] = project(normed, width)
    extended[0:rim, :] = jnp.zeros((rim, 3 * width), f32)
    for load in loads[3:7]:
        load.wait()

    @pl.when(me == 0)
    def _():
        long_taps[0 : med.shape[0], :] += med[...]
        long_taps[0:1, :] += skip_ref[...]

    sends[0] = long_taps[...].T.astype(bf16).reshape(sends.shape[1:])
    signal[...] = mix(1, 0, rows) * mix(2, 0, rows)
    turn_signal(rows // 2, rows // 2)
    pl.semaphore_wait(barrier, devices - 1)
    halo_copy = pltpu.make_async_remote_copy(
        src_ref=tokens.at[pl.ds(rows - rim, rim)],
        dst_ref=halo,
        send_sem=halo_sem.at[0],
        recv_sem=halo_sem.at[1],
        device_id={"seq": lax.rem(me + 1, devices)},
        device_id_type=pl.DeviceIdType.MESH,
    )

    @pl.when(me < devices - 1)
    def _():
        halo_copy.start()

    scatter(0)

    @pl.when(me > 0)
    def _():
        halo_copy.wait_recv()
        extended[0:rim, :] = project(rms_normed(halo[...], gain_ref[...]), 0)
        signal[0:rim, :] = mix(1, 0, rim) * mix(2, 0, rim)

    turn_signal(0, rows // 2)
    scatter(1)

    extended[rim:, :width] = dot(normed, w_in[:, :width]).astype(bf16).astype(f32)
    query = mix(0, 0, rows).T
    for load in loads[7:]:
        load.wait()

    def spectrum(block, first, turns):
        part = dot(first[...], block)
        re, im = part[:width], part[width:]
        cos_t, sin_t = turns[:width], turns[width:]
        turned = jnp.concatenate([re * cos_t + im * sin_t, im * cos_t - re * sin_t], axis=1)
        spec = dot(turned.astype(bf16), middle[...])
        return spec[:, :rows], spec[:, rows:]

    def inverse(sig, gain, turns, last):
        (sr, si), (gr, gi) = sig, gain
        prod = jnp.concatenate([sr * gi + si * gr, sr * gr - si * gi], axis=1)
        back = dot(prod.astype(bf16), middle[...])
        im, re = back[:, :rows], back[:, rows:]
        cos_t, sin_t = turns[:width], turns[width:]
        turned = jnp.concatenate([re * cos_t - im * sin_t, re * sin_t + im * cos_t], axis=0)
        return dot(last[...], turned.astype(bf16)).astype(bf16)

    def joined(kind, which):
        front = from_front[kind, :, which].reshape(half, rows)
        return jnp.concatenate([front, from_back[kind].reshape(half, rows)], axis=0)

    def finish():
        gated = (query * results[...].reshape(width, rows).astype(f32)).astype(bf16).T
        out_ref[...] = dot(gated, w_out[...]).astype(bf16)

    @pl.when(in_front)
    def _():
        received(from_front.at[0, pl.ds(0, side - 1)], 0)
        gain = spectrum(from_front[0].reshape(width, rows), front_first, front_turns)
        received(from_front.at[1, pl.ds(0, side - 1)], 2)
        sig = spectrum(from_front[1].reshape(width, rows), front_first, front_turns)
        front_out[...] = inverse(sig, gain, front_turns, front_last).reshape(front_out.shape)
        for d in same:
            remote(front_out.at[d], results.at[:, own], d, 4, 4).start()
        results[:, own] = front_out[own]
        received(from_back.at[0], 1)
        gain = spectrum(joined(0, 0), all_first, all_turns)
        received(from_back.at[1], 3)
        sig = spectrum(joined(1, 0), all_first, all_turns)
        back_out[...] = inverse(sig, gain, all_turns, all_last).reshape(back_out.shape)
        for d in cross:
            remote(back_out.at[d], results.at[0, own], side + d, 5, 4).start()
        received(results.at[:, pl.ds(0, side - 1)], 4)
        finish()
        for kind in range(2):
            sent(sends.at[kind, :, pl.ds(0, side - 1)], 2 * kind)
            sent(sends.at[kind, 1], 2 * kind + 1)
        sent(front_out.at[pl.ds(0, side - 1)], 4)
        sent(back_out, 5)

    @pl.when(jnp.logical_not(in_front))
    def _():
        received(from_front.at[0, :, 1], 0)
        received(from_back.at[0, pl.ds(0, side - 1)], 1)
        gain = spectrum(joined(0, 1), all_first, all_turns)
        received(from_front.at[1, :, 1], 2)
        received(from_back.at[1, pl.ds(0, side - 1)], 3)
        sig = spectrum(joined(1, 1), all_first, all_turns)
        back_out[...] = inverse(sig, gain, all_turns, all_last).reshape(back_out.shape)
        for d in same:
            remote(back_out.at[d], results.at[1, own], side + d, 5, 5).start()
        results[1, own] = back_out[own]
        received(results.at[0], 4)
        received(results.at[1, pl.ds(0, side - 1)], 5)
        finish()
        for kind in range(2):
            sent(sends.at[kind, 0], 2 * kind)
            sent(sends.at[kind, 1, pl.ds(0, side - 1)], 2 * kind + 1)
        sent(back_out.at[pl.ds(0, side - 1)], 5)

    @pl.when(me < devices - 1)
    def _():
        halo_copy.wait_send()


def fused(tokens, norm_gain, w_in, short_filter, long_filter, medium_filter, skip_gain, w_out):
    rows, width = tokens.shape
    devices = lax.axis_size("seq")
    side = devices // 2
    chans = width // devices
    all_first, middle, all_last, *all_turns = tables(devices, rows, chans)
    front_first, _, front_last, *front_turns = tables(side, rows, 2 * chans)
    consts = [
        all_first,
        np.concatenate(all_turns, axis=0),
        all_last[width // 2 :],
        front_first,
        np.concatenate(front_turns, axis=0),
        front_last,
        middle,
    ]
    rim = 16
    held = [
        tokens,
        norm_gain.reshape(1, width),
        w_in,
        short_filter,
        long_filter,
        medium_filter,
        skip_gain.reshape(1, width),
        w_out,
        *[jnp.asarray(t) for t in consts],
    ]
    return pl.pallas_call(
        functools.partial(kernel, devices),
        out_shape=pltpu.VMEM((rows, width), bf16),
        in_specs=[pl.BlockSpec(memory_space=pl.ANY)] * len(held),
        out_specs=pl.BlockSpec(memory_space=pltpu.VMEM),
        scratch_shapes=[pltpu.VMEM(a.shape, a.dtype) for a in held]
        + [
            pltpu.VMEM((rim, width), bf16),
            pltpu.VMEM((rim + rows, 3 * width), f32),
            pltpu.VMEM((rows, width), f32),
            pltpu.VMEM((2, 2, side, chans, rows), bf16),
            pltpu.VMEM((2, side, 2, chans, rows), bf16),
            pltpu.VMEM((2, side, chans, rows), bf16),
            pltpu.VMEM((side, 2, chans, rows), bf16),
            pltpu.VMEM((side, chans, rows), bf16),
            pltpu.VMEM((2, side, chans, rows), bf16),
            pltpu.SemaphoreType.DMA((len(held),)),
            pltpu.SemaphoreType.DMA((2,)),
            pltpu.SemaphoreType.DMA((6,)),
            pltpu.SemaphoreType.DMA((6,)),
        ],
        compiler_params=pltpu.CompilerParams(collective_id=0, has_side_effects=True),
    )(*held)


def solution(mesh):
    placed = (P(("groups", "seq"), None), P(), P(), P(), P("seq", None), P(), P(), P())

    def step(tokens, norm_gain, w_in, short_filter, long_filter, medium_filter, skip_gain, w_out):
        chans = tokens.shape[1] // mesh.shape["seq"]
        whole_tiles = chans == 16 and tokens.shape[0] == tokens.shape[1]
        body = fused if whole_tiles else local
        return body(tokens, norm_gain, w_in, short_filter, long_filter, medium_filter, skip_gain, w_out)

    return jax.shard_map(
        step, mesh=mesh, in_specs=placed, out_specs=P(("groups", "seq"), None), check_vma=False
    )
```

```python
import functools
import math

import jax
import jax.numpy as jnp
import numpy as np
from jax import lax
from jax.experimental import pallas as pl
from jax.experimental.pallas import tpu as pltpu
from jax.sharding import PartitionSpec as P

epsilon = 1e-06
bf16 = jnp.bfloat16
f32 = jnp.float32


def tables(devices, tok_rows, chans):
    full = devices * tok_rows
    idx = np.arange(devices)
    angle = 2.0 * math.pi * ((idx[:, None] * (4 * idx[None, :] + 1)) % (4 * devices)) / (4 * devices)
    eye = np.eye(chans)
    outer_cos = np.kron(np.cos(angle), eye)
    outer_sin = np.kron(np.sin(angle), eye)
    first = np.concatenate([outer_cos.T, -outer_sin.T], axis=0)
    last = np.concatenate([outer_cos, -outer_sin], axis=1) / full
    pos = np.arange(tok_rows)
    turn = 2.0 * math.pi * ((4 * idx[:, None] + 1) * pos[None, :]) / (4 * full)
    tw_cos = np.repeat(np.cos(turn), chans, axis=0)
    tw_sin = np.repeat(np.sin(turn), chans, axis=0)
    inner = 2.0 * math.pi * (pos[:, None] * pos[None, :] % tok_rows) / tok_rows
    cos_t, sin_t = np.cos(inner), np.sin(inner)
    middle = np.block([[cos_t, -sin_t], [sin_t, cos_t]])
    return (
        first.astype(bf16),
        middle.astype(bf16),
        last.astype(bf16),
        tw_cos.astype(np.float32),
        tw_sin.astype(np.float32),
    )


def dot(a, b):
    return jnp.dot(a, b, preferred_element_type=f32)


def forward(rows, first, middle, tw_cos, tw_sin):
    half = rows.shape[0]
    part = dot(first, rows)
    re, im = part[:half], part[half:]
    turned = jnp.concatenate([re * tw_cos + im * tw_sin, im * tw_cos - re * tw_sin], axis=1)
    return dot(turned.astype(bf16), middle)


def convolve(sig, fil, first, middle, last, tw_cos, tw_sin):
    width = sig.shape[1]
    spec = forward(sig, first, middle, tw_cos, tw_sin)
    gain = forward(fil, first, middle, tw_cos, tw_sin)
    sr, si, gr, gi = spec[:, :width], spec[:, width:], gain[:, :width], gain[:, width:]
    prod = jnp.concatenate([sr * gi + si * gr, sr * gr - si * gi], axis=1).astype(bf16)
    back = dot(prod, middle)
    im, re = back[:, :width], back[:, width:]
    turned = jnp.concatenate([re * tw_cos - im * tw_sin, re * tw_sin + im * tw_cos], axis=0)
    return dot(last, turned.astype(bf16))


def from_behind(array, axis, by):
    devices = lax.axis_size(axis)
    pairs = [(i, i + by) for i in range(devices) if 0 <= i + by < devices]
    return lax.ppermute(array, axis, pairs)


def local(tokens, norm_gain, w_in, short_filter, long_filter, medium_filter, skip_gain, w_out):
    tok_rows, chan_width = tokens.shape
    devices = lax.axis_size("seq")
    my_index = lax.axis_index("seq")
    chans = chan_width // devices
    consts = [jnp.asarray(t) for t in tables(devices, tok_rows, chans)]
    med = jnp.pad(medium_filter, ((0, tok_rows - medium_filter.shape[0]), (0, 0)))
    med = med.at[0].add(skip_gain)
    taps = (long_filter + jnp.where(my_index == 0, med, 0.0)).astype(bf16)
    inputs = tokens.astype(f32)
    mean_sq = jnp.mean(inputs * inputs, axis=-1, keepdims=True)
    normed = (inputs * lax.rsqrt(mean_sq + epsilon) * norm_gain).astype(bf16)
    projected = dot(normed, w_in).astype(bf16)
    taps_count = short_filter.shape[0]
    rim_rows = from_behind(projected[tok_rows - (taps_count - 1) :], "seq", 1)
    extended = jnp.concatenate([rim_rows, projected], axis=0)
    short_mix = jnp.zeros((tok_rows, projected.shape[1]), f32)
    for tap_num in range(taps_count):
        begin = taps_count - 1 - tap_num
        short_mix = short_mix + short_filter[tap_num] * extended[begin : begin + tok_rows]
    query_part = short_mix[:, 0:chan_width]
    signal = short_mix[:, chan_width : 2 * chan_width] * short_mix[:, 2 * chan_width :]

    def spread(array):
        split = array.astype(bf16).T.reshape(devices, chans, tok_rows)
        return lax.all_to_all(split, "seq", 0, 0, tiled=True).reshape(chan_width, tok_rows)

    mixed = convolve(spread(signal), spread(taps), *consts)
    back = spread_back(mixed, devices, chans)
    mixed_out = (query_part * back.T.astype(f32)).astype(bf16)
    return dot(mixed_out, w_out).astype(bf16)


def spread_back(mixed, devices, chans):
    split = mixed.astype(bf16).reshape(devices, chans, mixed.shape[1])
    return lax.all_to_all(split, "seq", 0, 0, tiled=True).reshape(mixed.shape)


def rms_normed(rows, gain):
    rows = rows.astype(f32)
    mean_sq = jnp.mean(rows * rows, axis=-1, keepdims=True)
    return (rows * lax.rsqrt(mean_sq + epsilon) * gain).astype(bf16)


def relative(own, count):
    steps = []
    bit = 1
    while bit < count:
        steps.append((bit, bit * (1 - 2 * (own // bit % 2))))
        bit *= 2
    return [own + sum(step for bit, step in steps if off // bit % 2) for off in range(count - 1, -1, -1)]


def kernel(
    devices,
    tokens_hbm,
    gain_hbm,
    w_in_hbm,
    short_hbm,
    long_hbm,
    med_hbm,
    skip_hbm,
    w_out_hbm,
    all_first_hbm,
    all_turns_hbm,
    all_last_hbm,
    front_first_hbm,
    front_turns_hbm,
    front_last_hbm,
    middle_hbm,
    out_ref,
    tokens,
    gain_ref,
    w_in,
    short_ref,
    long_taps,
    med,
    skip_ref,
    w_out,
    all_first,
    all_turns,
    all_last,
    front_first,
    front_turns,
    front_last,
    middle,
    halo,
    extended,
    signal,
    sends,
    from_front,
    from_back,
    front_out,
    back_out,
    results,
    ready,
    local_sem,
    halo_sem,
    send_sem,
    recv_sem,
):
    me = lax.axis_index("seq")
    rows, width = tokens.shape
    side = devices // 2
    chans = width // devices
    half = width // 2
    in_front = me < side
    own = lax.rem(me, side)
    cross = relative(own, side)
    same = cross[:-1]
    rim = halo.shape[0]
    in_back = jnp.logical_not(in_front)
    barrier = pltpu.get_barrier_semaphore()

    def announce(semaphore, peer):
        pl.semaphore_signal(
            semaphore, inc=1, device_id={"seq": peer}, device_id_type=pl.DeviceIdType.MESH
        )

    @pl.when(in_front)
    def _():
        for d in same:
            announce(barrier, d)
        for d in cross:
            announce(barrier, side + d)

    @pl.when(in_back)
    def _():
        for d in same:
            announce(barrier, side + d)

    loads = [
        pltpu.make_async_copy(source, target, local_sem.at[num])
        for num, (source, target) in enumerate(
            [
                (tokens_hbm, tokens),
                (gain_hbm, gain_ref),
                (w_in_hbm, w_in),
                (short_hbm, short_ref),
                (long_hbm, long_taps),
                (med_hbm, med),
                (skip_hbm, skip_ref),
                (middle_hbm, middle),
                (front_first_hbm, front_first),
                (front_turns_hbm, front_turns),
                (front_last_hbm, front_last),
                (all_first_hbm, all_first),
                (all_turns_hbm, all_turns),
                (all_last_hbm, all_last),
                (w_out_hbm, w_out),
            ]
        )
    ]
    for load in loads:
        load.start()

    @pl.when(me == devices - 1)
    def _():
        pl.semaphore_wait(barrier, devices - 1)
        for d in cross:
            announce(ready, d)

    def remote(source, target, peer, sent, received):
        return pltpu.make_async_remote_copy(
            src_ref=source,
            dst_ref=target,
            send_sem=send_sem.at[sent],
            recv_sem=recv_sem.at[received],
            device_id={"seq": peer},
            device_id_type=pl.DeviceIdType.MESH,
        )

    def received(ref, num):
        remote(ref, ref, 0, num, num).wait_recv()

    def sent(ref, num):
        remote(ref, ref, 0, num, num).wait_send()

    def same_from_front(kind):
        for d in same:
            remote(sends.at[kind, :, d], from_front.at[kind, own], d, 2 * kind, 2 * kind).start()
        from_front[kind, own] = sends[kind, :, own]

    def cross_from_front(kind):
        for d in cross:
            target = from_front.at[kind, own, 1]
            remote(sends.at[kind, 1, d], target, side + d, 2 * kind + 1, 2 * kind).start()

    def same_from_back(kind):
        for d in same:
            target = from_back.at[kind, own]
            remote(sends.at[kind, 1, d], target, side + d, 2 * kind + 1, 2 * kind + 1).start()
        from_back[kind, own] = sends[kind, 1, own]

    def cross_from_back(kind):
        for d in cross:
            target = from_back.at[kind, own]
            remote(sends.at[kind, 0, d], target, d, 2 * kind, 2 * kind + 1).start()

    def project(part_normed, begin):
        return dot(part_normed, w_in[:, begin:]).astype(bf16).astype(f32)

    def mix(part, begin, count):
        cols = pl.ds(part * width, width)
        total = short_ref[0:1, cols] * extended[rim + begin : rim + begin + count, cols]
        for tap in range(1, short_ref.shape[0]):
            start = rim + begin - tap
            total = total + short_ref[tap : tap + 1, cols] * extended[start : start + count, cols]
        return total

    def turn_signal(begin, count):
        block = signal[begin : begin + count, :].T.astype(bf16)
        sends[1, :, :, :, begin : begin + count] = block.reshape(2, side, chans, count)

    for load in loads[:3]:
        load.wait()
    normed = rms_normed(tokens[...], gain_ref[...])
    extended[rim:, width:] = project(normed, width)
    extended[0:rim, :] = jnp.zeros((rim, 3 * width), f32)
    for load in loads[3:7]:
        load.wait()

    @pl.when(me == 0)
    def _():
        long_taps[0 : med.shape[0], :] += med[...]
        long_taps[0:1, :] += skip_ref[...]

    sends[0] = long_taps[...].T.astype(bf16).reshape(sends.shape[1:])
    signal[...] = mix(1, 0, rows) * mix(2, 0, rows)
    turn_signal(rows // 2, rows // 2)
    halo_copy = pltpu.make_async_remote_copy(
        src_ref=tokens.at[pl.ds(rows - rim, rim)],
        dst_ref=halo,
        send_sem=halo_sem.at[0],
        recv_sem=halo_sem.at[1],
        device_id={"seq": lax.rem(me + 1, devices)},
        device_id_type=pl.DeviceIdType.MESH,
    )

    @pl.when(in_front)
    def _():
        pl.semaphore_wait(barrier, side - 1)

        @pl.when(me < side - 1)
        def _():
            halo_copy.start()

        same_from_front(0)

    @pl.when(in_back)
    def _():
        @pl.when(me < devices - 1)
        def _():
            pl.semaphore_wait(barrier, devices - 1)
            halo_copy.start()

        same_from_back(0)
        cross_from_back(0)

    @pl.when(me > 0)
    def _():
        halo_copy.wait_recv()
        extended[0:rim, :] = project(rms_normed(halo[...], gain_ref[...]), 0)
        signal[0:rim, :] = mix(1, 0, rim) * mix(2, 0, rim)

    turn_signal(0, rows // 2)

    @pl.when(in_front)
    def _():
        same_from_front(1)
        pl.semaphore_wait(ready, 1)

        @pl.when(me == side - 1)
        def _():
            halo_copy.start()

        cross_from_front(0)
        cross_from_front(1)

    @pl.when(in_back)
    def _():
        same_from_back(1)
        cross_from_back(1)

    extended[rim:, :width] = dot(normed, w_in[:, :width]).astype(bf16).astype(f32)
    query = mix(0, 0, rows).T
    for load in loads[7:]:
        load.wait()

    def spectrum(block, first, turns):
        part = dot(first[...], block)
        re, im = part[:width], part[width:]
        cos_t, sin_t = turns[:width], turns[width:]
        turned = jnp.concatenate([re * cos_t + im * sin_t, im * cos_t - re * sin_t], axis=1)
        spec = dot(turned.astype(bf16), middle[...])
        return spec[:, :rows], spec[:, rows:]

    def inverse(sig, gain, turns, last):
        (sr, si), (gr, gi) = sig, gain
        prod = jnp.concatenate([sr * gi + si * gr, sr * gr - si * gi], axis=1)
        back = dot(prod.astype(bf16), middle[...])
        im, re = back[:, :rows], back[:, rows:]
        cos_t, sin_t = turns[:width], turns[width:]
        turned = jnp.concatenate([re * cos_t - im * sin_t, re * sin_t + im * cos_t], axis=0)
        return dot(last[...], turned.astype(bf16)).astype(bf16)

    def joined(kind, which):
        front = from_front[kind, :, which].reshape(half, rows)
        return jnp.concatenate([front, from_back[kind].reshape(half, rows)], axis=0)

    def finish():
        gated = (query * results[...].reshape(width, rows).astype(f32)).astype(bf16).T
        out_ref[...] = dot(gated, w_out[...]).astype(bf16)

    @pl.when(in_front)
    def _():
        received(from_front.at[0, pl.ds(0, side - 1)], 0)
        gain = spectrum(from_front[0].reshape(width, rows), front_first, front_turns)
        received(from_back.at[0], 1)
        back_gain = spectrum(joined(0, 0), all_first, all_turns)
        received(from_front.at[1, pl.ds(0, side - 1)], 2)
        sig = spectrum(from_front[1].reshape(width, rows), front_first, front_turns)
        front_out[...] = inverse(sig, gain, front_turns, front_last).reshape(front_out.shape)
        for d in same:
            remote(front_out.at[d], results.at[:, own], d, 4, 4).start()
        results[:, own] = front_out[own]
        received(from_back.at[1], 3)
        sig = spectrum(joined(1, 0), all_first, all_turns)
        back_out[...] = inverse(sig, back_gain, all_turns, all_last).reshape(back_out.shape)
        for d in cross:
            remote(back_out.at[d], results.at[0, own], side + d, 5, 4).start()
        received(results.at[:, pl.ds(0, side - 1)], 4)
        finish()
        for kind in range(2):
            sent(sends.at[kind, :, pl.ds(0, side - 1)], 2 * kind)
            sent(sends.at[kind, 1], 2 * kind + 1)
        sent(front_out.at[pl.ds(0, side - 1)], 4)
        sent(back_out, 5)

    @pl.when(jnp.logical_not(in_front))
    def _():
        received(from_front.at[0, :, 1], 0)
        received(from_back.at[0, pl.ds(0, side - 1)], 1)
        gain = spectrum(joined(0, 1), all_first, all_turns)
        received(from_front.at[1, :, 1], 2)
        received(from_back.at[1, pl.ds(0, side - 1)], 3)
        sig = spectrum(joined(1, 1), all_first, all_turns)
        back_out[...] = inverse(sig, gain, all_turns, all_last).reshape(back_out.shape)
        for d in same:
            remote(back_out.at[d], results.at[1, own], side + d, 5, 5).start()
        results[1, own] = back_out[own]
        received(results.at[0], 4)
        received(results.at[1, pl.ds(0, side - 1)], 5)
        finish()
        for kind in range(2):
            sent(sends.at[kind, 0], 2 * kind)
            sent(sends.at[kind, 1, pl.ds(0, side - 1)], 2 * kind + 1)
        sent(back_out.at[pl.ds(0, side - 1)], 5)

    @pl.when(me < devices - 1)
    def _():
        halo_copy.wait_send()


def fused(tokens, norm_gain, w_in, short_filter, long_filter, medium_filter, skip_gain, w_out):
    rows, width = tokens.shape
    devices = lax.axis_size("seq")
    side = devices // 2
    chans = width // devices
    all_first, middle, all_last, *all_turns = tables(devices, rows, chans)
    front_first, _, front_last, *front_turns = tables(side, rows, 2 * chans)
    consts = [
        all_first,
        np.concatenate(all_turns, axis=0),
        all_last[width // 2 :],
        front_first,
        np.concatenate(front_turns, axis=0),
        front_last,
        middle,
    ]
    rim = 16
    held = [
        tokens,
        norm_gain.reshape(1, width),
        w_in,
        short_filter,
        long_filter,
        medium_filter,
        skip_gain.reshape(1, width),
        w_out,
        *[jnp.asarray(t) for t in consts],
    ]
    return pl.pallas_call(
        functools.partial(kernel, devices),
        out_shape=pltpu.VMEM((rows, width), bf16),
        in_specs=[pl.BlockSpec(memory_space=pl.ANY)] * len(held),
        out_specs=pl.BlockSpec(memory_space=pltpu.VMEM),
        scratch_shapes=[pltpu.VMEM(a.shape, a.dtype) for a in held]
        + [
            pltpu.VMEM((rim, width), bf16),
            pltpu.VMEM((rim + rows, 3 * width), f32),
            pltpu.VMEM((rows, width), f32),
            pltpu.VMEM((2, 2, side, chans, rows), bf16),
            pltpu.VMEM((2, side, 2, chans, rows), bf16),
            pltpu.VMEM((2, side, chans, rows), bf16),
            pltpu.VMEM((side, 2, chans, rows), bf16),
            pltpu.VMEM((side, chans, rows), bf16),
            pltpu.VMEM((2, side, chans, rows), bf16),
            pltpu.SemaphoreType.REGULAR,
            pltpu.SemaphoreType.DMA((len(held),)),
            pltpu.SemaphoreType.DMA((2,)),
            pltpu.SemaphoreType.DMA((6,)),
            pltpu.SemaphoreType.DMA((6,)),
        ],
        compiler_params=pltpu.CompilerParams(collective_id=0, has_side_effects=True),
    )(*held)


def solution(mesh):
    placed = (P(("groups", "seq"), None), P(), P(), P(), P("seq", None), P(), P(), P())

    def step(tokens, norm_gain, w_in, short_filter, long_filter, medium_filter, skip_gain, w_out):
        chans = tokens.shape[1] // mesh.shape["seq"]
        whole_tiles = chans == 16 and tokens.shape[0] == tokens.shape[1]
        body = fused if whole_tiles else local
        return body(tokens, norm_gain, w_in, short_filter, long_filter, medium_filter, skip_gain, w_out)

    return jax.shard_map(
        step, mesh=mesh, in_specs=placed, out_specs=P(("groups", "seq"), None), check_vma=False
    )
```

```python
import functools
import math

import jax
import jax.numpy as jnp
import numpy as np
from jax import lax
from jax.experimental import pallas as pl
from jax.experimental.pallas import tpu as pltpu
from jax.sharding import PartitionSpec as P

epsilon = 1e-06
bf16 = jnp.bfloat16
f32 = jnp.float32


def tables(devices, tok_rows, chans):
    full = devices * tok_rows
    idx = np.arange(devices)
    angle = 2.0 * math.pi * ((idx[:, None] * (4 * idx[None, :] + 1)) % (4 * devices)) / (4 * devices)
    eye = np.eye(chans)
    outer_cos = np.kron(np.cos(angle), eye)
    outer_sin = np.kron(np.sin(angle), eye)
    first = np.concatenate([outer_cos.T, -outer_sin.T], axis=0)
    last = np.concatenate([outer_cos, -outer_sin], axis=1) / full
    pos = np.arange(tok_rows)
    turn = 2.0 * math.pi * ((4 * idx[:, None] + 1) * pos[None, :]) / (4 * full)
    tw_cos = np.repeat(np.cos(turn), chans, axis=0)
    tw_sin = np.repeat(np.sin(turn), chans, axis=0)
    inner = 2.0 * math.pi * (pos[:, None] * pos[None, :] % tok_rows) / tok_rows
    cos_t, sin_t = np.cos(inner), np.sin(inner)
    middle = np.block([[cos_t, -sin_t], [sin_t, cos_t]])
    return (
        first.astype(bf16),
        middle.astype(bf16),
        last.astype(bf16),
        tw_cos.astype(np.float32),
        tw_sin.astype(np.float32),
    )


def dot(a, b):
    return jnp.dot(a, b, preferred_element_type=f32)


def forward(rows, first, middle, tw_cos, tw_sin):
    half = rows.shape[0]
    part = dot(first, rows)
    re, im = part[:half], part[half:]
    turned = jnp.concatenate([re * tw_cos + im * tw_sin, im * tw_cos - re * tw_sin], axis=1)
    return dot(turned.astype(bf16), middle)


def convolve(sig, fil, first, middle, last, tw_cos, tw_sin):
    width = sig.shape[1]
    spec = forward(sig, first, middle, tw_cos, tw_sin)
    gain = forward(fil, first, middle, tw_cos, tw_sin)
    sr, si, gr, gi = spec[:, :width], spec[:, width:], gain[:, :width], gain[:, width:]
    prod = jnp.concatenate([sr * gi + si * gr, sr * gr - si * gi], axis=1).astype(bf16)
    back = dot(prod, middle)
    im, re = back[:, :width], back[:, width:]
    turned = jnp.concatenate([re * tw_cos - im * tw_sin, re * tw_sin + im * tw_cos], axis=0)
    return dot(last, turned.astype(bf16))


def from_behind(array, axis, by):
    devices = lax.axis_size(axis)
    pairs = [(i, i + by) for i in range(devices) if 0 <= i + by < devices]
    return lax.ppermute(array, axis, pairs)


def local(tokens, norm_gain, w_in, short_filter, long_filter, medium_filter, skip_gain, w_out):
    tok_rows, chan_width = tokens.shape
    devices = lax.axis_size("seq")
    my_index = lax.axis_index("seq")
    chans = chan_width // devices
    consts = [jnp.asarray(t) for t in tables(devices, tok_rows, chans)]
    med = jnp.pad(medium_filter, ((0, tok_rows - medium_filter.shape[0]), (0, 0)))
    med = med.at[0].add(skip_gain)
    taps = (long_filter + jnp.where(my_index == 0, med, 0.0)).astype(bf16)
    inputs = tokens.astype(f32)
    mean_sq = jnp.mean(inputs * inputs, axis=-1, keepdims=True)
    normed = (inputs * lax.rsqrt(mean_sq + epsilon) * norm_gain).astype(bf16)
    projected = dot(normed, w_in).astype(bf16)
    taps_count = short_filter.shape[0]
    rim_rows = from_behind(projected[tok_rows - (taps_count - 1) :], "seq", 1)
    extended = jnp.concatenate([rim_rows, projected], axis=0)
    short_mix = jnp.zeros((tok_rows, projected.shape[1]), f32)
    for tap_num in range(taps_count):
        begin = taps_count - 1 - tap_num
        short_mix = short_mix + short_filter[tap_num] * extended[begin : begin + tok_rows]
    query_part = short_mix[:, 0:chan_width]
    signal = short_mix[:, chan_width : 2 * chan_width] * short_mix[:, 2 * chan_width :]

    def spread(array):
        split = array.astype(bf16).T.reshape(devices, chans, tok_rows)
        return lax.all_to_all(split, "seq", 0, 0, tiled=True).reshape(chan_width, tok_rows)

    mixed = convolve(spread(signal), spread(taps), *consts)
    back = spread_back(mixed, devices, chans)
    mixed_out = (query_part * back.T.astype(f32)).astype(bf16)
    return dot(mixed_out, w_out).astype(bf16)


def spread_back(mixed, devices, chans):
    split = mixed.astype(bf16).reshape(devices, chans, mixed.shape[1])
    return lax.all_to_all(split, "seq", 0, 0, tiled=True).reshape(mixed.shape)


def rms_normed(rows, gain):
    rows = rows.astype(f32)
    mean_sq = jnp.mean(rows * rows, axis=-1, keepdims=True)
    return (rows * lax.rsqrt(mean_sq + epsilon) * gain).astype(bf16)


def relative(own, count):
    steps = []
    bit = 1
    while bit < count:
        steps.append((bit, bit * (1 - 2 * (own // bit % 2))))
        bit *= 2
    return [own + sum(step for bit, step in steps if off // bit % 2) for off in range(count - 1, -1, -1)]


def kernel(
    devices,
    tokens_hbm,
    gain_hbm,
    w_in_hbm,
    short_hbm,
    long_hbm,
    med_hbm,
    skip_hbm,
    w_out_hbm,
    all_first_hbm,
    all_turns_hbm,
    all_last_hbm,
    front_first_hbm,
    front_turns_hbm,
    front_last_hbm,
    middle_hbm,
    out_ref,
    tokens,
    gain_ref,
    w_in,
    short_ref,
    long_taps,
    med,
    skip_ref,
    w_out,
    all_first,
    all_turns,
    all_last,
    front_first,
    front_turns,
    front_last,
    middle,
    halo,
    extended,
    signal,
    later,
    sends,
    from_front,
    from_back,
    front_out,
    back_out,
    results,
    ready,
    local_sem,
    halo_sem,
    send_sem,
    recv_sem,
):
    me = lax.axis_index("seq")
    rows, width = tokens.shape
    side = devices // 2
    chans = width // devices
    half = width // 2
    lanes = rows // 2
    fine = chans // 2
    in_front = me < side
    own = lax.rem(me, side)
    cross = relative(own, side)
    same = cross[:-1]
    rim = halo.shape[0]
    in_back = jnp.logical_not(in_front)
    barrier = pltpu.get_barrier_semaphore()

    def announce(semaphore, peer):
        pl.semaphore_signal(
            semaphore, inc=1, device_id={"seq": peer}, device_id_type=pl.DeviceIdType.MESH
        )

    @pl.when(in_front)
    def _():
        for d in same:
            announce(barrier, d)
        for d in cross:
            announce(barrier, side + d)

    @pl.when(in_back)
    def _():
        for d in same:
            announce(barrier, side + d)

    loads = [
        pltpu.make_async_copy(source, target, local_sem.at[num])
        for num, (source, target) in enumerate(
            [
                (long_hbm, long_taps),
                (med_hbm, med),
                (skip_hbm, skip_ref),
                (tokens_hbm, tokens),
                (gain_hbm, gain_ref),
                (w_in_hbm, w_in),
                (short_hbm, short_ref),
                (middle_hbm, middle),
                (front_first_hbm, front_first),
                (front_turns_hbm, front_turns),
                (front_last_hbm, front_last),
                (all_first_hbm, all_first),
                (all_turns_hbm, all_turns),
                (all_last_hbm, all_last),
                (w_out_hbm, w_out),
            ]
        )
    ]
    for load in loads[:7]:
        load.start()

    @pl.when(me == devices - 1)
    def _():
        pl.semaphore_wait(barrier, devices - 1)
        for d in cross:
            announce(ready, d)

    def remote(source, target, peer, sent, received):
        return pltpu.make_async_remote_copy(
            src_ref=source,
            dst_ref=target,
            send_sem=send_sem.at[sent],
            recv_sem=recv_sem.at[received],
            device_id={"seq": peer},
            device_id_type=pl.DeviceIdType.MESH,
        )

    def received(ref, num):
        remote(ref, ref, 0, num, num).wait_recv()

    def sent(ref, num):
        remote(ref, ref, 0, num, num).wait_send()

    def same_from_front(kind):
        for d in same:
            remote(sends.at[kind, :, d], from_front.at[kind, own], d, 2 * kind, 2 * kind).start()
        from_front[kind, own] = sends[kind, :, own]

    def cross_from_front(kind):
        for d in cross:
            target = from_front.at[kind, own, 1]
            remote(sends.at[kind, 1, d], target, side + d, 2 * kind + 1, 2 * kind).start()

    def same_from_back(kind):
        for d in same:
            target = from_back.at[kind, own]
            remote(sends.at[kind, 1, d], target, side + d, 2 * kind + 1, 2 * kind + 1).start()
        from_back[kind, own] = sends[kind, 1, own]

    def cross_from_back(kind):
        for d in cross:
            target = from_back.at[kind, own]
            remote(sends.at[kind, 0, d], target, d, 2 * kind, 2 * kind + 1).start()

    def project(part_normed, begin):
        return dot(part_normed, w_in[:, begin:]).astype(bf16).astype(f32)

    def mix(part, begin, count):
        cols = pl.ds(part * width, width)
        total = short_ref[0:1, cols] * extended[rim + begin : rim + begin + count, cols]
        for tap in range(1, short_ref.shape[0]):
            start = rim + begin - tap
            total = total + short_ref[tap : tap + 1, cols] * extended[start : start + count, cols]
        return total

    def turn(ref, begin):
        block = ref[begin : begin + lanes, :].T.reshape(2, side, 2, fine, lanes)
        return jnp.concatenate([block[:, :, 0], block[:, :, 1]], axis=3)

    halo_copy = pltpu.make_async_remote_copy(
        src_ref=tokens.at[pl.ds(rows - rim, rim)],
        dst_ref=halo,
        send_sem=halo_sem.at[0],
        recv_sem=halo_sem.at[1],
        device_id={"seq": lax.rem(me + 1, devices)},
        device_id_type=pl.DeviceIdType.MESH,
    )
    for load in loads[:3]:
        load.wait()

    @pl.when(me == 0)
    def _():
        long_taps[0 : med.shape[0], :] += med[...]
        long_taps[0:1, :] += skip_ref[...]

    sends[0] = jnp.concatenate([turn(long_taps, 0), turn(long_taps, lanes)], axis=2).astype(bf16)
    loads[3].wait()

    @pl.when(in_back)
    def _():
        @pl.when(me < devices - 1)
        def _():
            pl.semaphore_wait(barrier, devices - 1)
            halo_copy.start()

        same_from_back(0)
        cross_from_back(0)

    for load in loads[7:]:
        load.start()
    for load in loads[4:7]:
        load.wait()
    normed = rms_normed(tokens[...], gain_ref[...])
    extended[rim:, width:] = project(normed, width)
    extended[0:rim, :] = jnp.zeros((rim, 3 * width), f32)
    signal[...] = mix(1, 0, rows) * mix(2, 0, rows)
    later[...] = turn(signal, lanes)

    @pl.when(in_front)
    def _():
        pl.semaphore_wait(barrier, side - 1)

        @pl.when(me < side - 1)
        def _():
            halo_copy.start()

        same_from_front(0)

    @pl.when(me > 0)
    def _():
        halo_copy.wait_recv()
        extended[0:rim, :] = project(rms_normed(halo[...], gain_ref[...]), 0)
        signal[0:rim, :] = mix(1, 0, rim) * mix(2, 0, rim)

    sends[1] = jnp.concatenate([turn(signal, 0), later[...]], axis=2).astype(bf16)

    @pl.when(in_front)
    def _():
        same_from_front(1)
        pl.semaphore_wait(ready, 1)

        @pl.when(me == side - 1)
        def _():
            halo_copy.start()

        cross_from_front(0)
        cross_from_front(1)

    @pl.when(in_back)
    def _():
        same_from_back(1)
        cross_from_back(1)

    extended[rim:, :width] = dot(normed, w_in[:, :width]).astype(bf16).astype(f32)
    query = mix(0, 0, rows).T
    for load in loads[7:]:
        load.wait()

    def stacked(left, right):
        pieces = [(left[:, :lanes], right[:, :lanes]), (left[:, lanes:], right[:, lanes:])]
        return jnp.concatenate([jnp.concatenate(pair, axis=1) for pair in pieces], axis=0)

    def spread(array):
        return jnp.concatenate([array[:width], array[width:]], axis=1)

    def spectrum(block, first, turns):
        part = dot(first[...], block)
        re, im = part[:width], part[width:]
        cos_t, sin_t = turns[:width], turns[width:]
        turned = stacked(re * cos_t + im * sin_t, im * cos_t - re * sin_t)
        spec = dot(turned.astype(bf16), middle[...])
        return spec[:, :lanes], spec[:, lanes:]

    def inverse(sig, gain, turns, last):
        (sr, si), (gr, gi) = sig, gain
        prod = jnp.concatenate([sr * gi + si * gr, sr * gr - si * gi], axis=1)
        back = dot(prod.astype(bf16), middle[...])
        im, re = spread(back[:, :lanes]), spread(back[:, lanes:])
        cos_t, sin_t = turns[:width], turns[width:]
        turned = jnp.concatenate([re * cos_t - im * sin_t, re * sin_t + im * cos_t], axis=0)
        return dot(last[...], turned.astype(bf16)).astype(bf16)

    def joined(kind, which):
        front = from_front[kind, :, which].reshape(half, rows)
        return jnp.concatenate([front, from_back[kind].reshape(half, rows)], axis=0)

    def finish():
        mixed = results[...].astype(f32)
        early, late = mixed[:, :, :fine], mixed[:, :, fine:]
        sides = [
            jnp.concatenate([early[:, :, :, cut], late[:, :, :, cut]], axis=3)
            for cut in (slice(0, lanes), slice(lanes, rows))
        ]
        mixed = jnp.concatenate(sides, axis=2).reshape(width, rows)
        gated = (query * mixed).astype(bf16).T
        out_ref[...] = dot(gated, w_out[...]).astype(bf16)

    @pl.when(in_front)
    def _():
        received(from_front.at[0, pl.ds(0, side - 1)], 0)
        gain = spectrum(from_front[0].reshape(width, rows), front_first, front_turns)
        received(from_front.at[1, pl.ds(0, side - 1)], 2)
        sig = spectrum(from_front[1].reshape(width, rows), front_first, front_turns)
        front_out[...] = inverse(sig, gain, front_turns, front_last).reshape(front_out.shape)
        for d in same:
            remote(front_out.at[d], results.at[:, own], d, 4, 4).start()
        results[:, own] = front_out[own]
        received(from_back.at[0], 1)
        back_gain = spectrum(joined(0, 0), all_first, all_turns)
        received(from_back.at[1], 3)
        sig = spectrum(joined(1, 0), all_first, all_turns)
        back_out[...] = inverse(sig, back_gain, all_turns, all_last).reshape(back_out.shape)
        for d in cross:
            remote(back_out.at[d], results.at[0, own], side + d, 5, 4).start()
        received(results.at[:, pl.ds(0, side - 1)], 4)
        finish()
        for kind in range(2):
            sent(sends.at[kind, :, pl.ds(0, side - 1)], 2 * kind)
            sent(sends.at[kind, 1], 2 * kind + 1)
        sent(front_out.at[pl.ds(0, side - 1)], 4)
        sent(back_out, 5)

    @pl.when(jnp.logical_not(in_front))
    def _():
        received(from_front.at[0, :, 1], 0)
        received(from_back.at[0, pl.ds(0, side - 1)], 1)
        gain = spectrum(joined(0, 1), all_first, all_turns)
        received(from_front.at[1, :, 1], 2)
        received(from_back.at[1, pl.ds(0, side - 1)], 3)
        sig = spectrum(joined(1, 1), all_first, all_turns)
        back_out[...] = inverse(sig, gain, all_turns, all_last).reshape(back_out.shape)
        for d in same:
            remote(back_out.at[d], results.at[1, own], side + d, 5, 5).start()
        results[1, own] = back_out[own]
        received(results.at[0], 4)
        received(results.at[1, pl.ds(0, side - 1)], 5)
        finish()
        for kind in range(2):
            sent(sends.at[kind, 0], 2 * kind)
            sent(sends.at[kind, 1, pl.ds(0, side - 1)], 2 * kind + 1)
        sent(back_out.at[pl.ds(0, side - 1)], 5)

    @pl.when(me < devices - 1)
    def _():
        halo_copy.wait_send()


def fused(tokens, norm_gain, w_in, short_filter, long_filter, medium_filter, skip_gain, w_out):
    rows, width = tokens.shape
    devices = lax.axis_size("seq")
    side = devices // 2
    chans = width // devices
    lanes, fine = rows // 2, chans // 2
    all_first, middle, all_last, *all_turns = tables(2 * devices, lanes, fine)
    front_first, _, front_last, *front_turns = tables(devices, lanes, chans)
    order = np.arange(width).reshape(side, 2, 2, fine).transpose(0, 2, 1, 3).reshape(-1)
    consts = [
        all_first,
        np.tile(np.concatenate(all_turns, axis=0), (1, 2)),
        all_last[width // 2 :],
        front_first[:, order],
        np.tile(np.concatenate(front_turns, axis=0), (1, 2)),
        front_last[order],
        middle,
    ]
    rim = 16
    held = [
        tokens,
        norm_gain.reshape(1, width),
        w_in,
        short_filter,
        long_filter,
        medium_filter,
        skip_gain.reshape(1, width),
        w_out,
        *[jnp.asarray(t) for t in consts],
    ]
    return pl.pallas_call(
        functools.partial(kernel, devices),
        out_shape=pltpu.VMEM((rows, width), bf16),
        in_specs=[pl.BlockSpec(memory_space=pl.ANY)] * len(held),
        out_specs=pl.BlockSpec(memory_space=pltpu.VMEM),
        scratch_shapes=[pltpu.VMEM(a.shape, a.dtype) for a in held]
        + [
            pltpu.VMEM((rim, width), bf16),
            pltpu.VMEM((rim + rows, 3 * width), f32),
            pltpu.VMEM((rows, width), f32),
            pltpu.VMEM((2, side, fine, rows), f32),
            pltpu.VMEM((2, 2, side, chans, rows), bf16),
            pltpu.VMEM((2, side, 2, chans, rows), bf16),
            pltpu.VMEM((2, side, chans, rows), bf16),
            pltpu.VMEM((side, 2, chans, rows), bf16),
            pltpu.VMEM((side, chans, rows), bf16),
            pltpu.VMEM((2, side, chans, rows), bf16),
            pltpu.SemaphoreType.REGULAR,
            pltpu.SemaphoreType.DMA((len(held),)),
            pltpu.SemaphoreType.DMA((2,)),
            pltpu.SemaphoreType.DMA((6,)),
            pltpu.SemaphoreType.DMA((6,)),
        ],
        compiler_params=pltpu.CompilerParams(collective_id=0, has_side_effects=True),
    )(*held)


def solution(mesh):
    placed = (P(("groups", "seq"), None), P(), P(), P(), P("seq", None), P(), P(), P())

    def step(tokens, norm_gain, w_in, short_filter, long_filter, medium_filter, skip_gain, w_out):
        chans = tokens.shape[1] // mesh.shape["seq"]
        whole_tiles = chans == 16 and tokens.shape[0] == tokens.shape[1]
        body = fused if whole_tiles else local
        return body(tokens, norm_gain, w_in, short_filter, long_filter, medium_filter, skip_gain, w_out)

    return jax.shard_map(
        step, mesh=mesh, in_specs=placed, out_specs=P(("groups", "seq"), None), check_vma=False
    )
```

```python
import functools
import math

import jax
import jax.numpy as jnp
import numpy as np
from jax import lax
from jax.experimental import pallas as pl
from jax.experimental.pallas import tpu as pltpu
from jax.sharding import PartitionSpec as P

epsilon = 1e-06
bf16 = jnp.bfloat16
f32 = jnp.float32


def tables(devices, tok_rows, chans):
    full = devices * tok_rows
    idx = np.arange(devices)
    angle = 2.0 * math.pi * ((idx[:, None] * (4 * idx[None, :] + 1)) % (4 * devices)) / (4 * devices)
    eye = np.eye(chans)
    outer_cos = np.kron(np.cos(angle), eye)
    outer_sin = np.kron(np.sin(angle), eye)
    first = np.concatenate([outer_cos.T, -outer_sin.T], axis=0)
    last = np.concatenate([outer_cos, -outer_sin], axis=1) / full
    pos = np.arange(tok_rows)
    turn = 2.0 * math.pi * ((4 * idx[:, None] + 1) * pos[None, :]) / (4 * full)
    tw_cos = np.repeat(np.cos(turn), chans, axis=0)
    tw_sin = np.repeat(np.sin(turn), chans, axis=0)
    inner = 2.0 * math.pi * (pos[:, None] * pos[None, :] % tok_rows) / tok_rows
    cos_t, sin_t = np.cos(inner), np.sin(inner)
    middle = np.block([[cos_t, -sin_t], [sin_t, cos_t]])
    return (
        first.astype(bf16),
        middle.astype(bf16),
        last.astype(bf16),
        tw_cos.astype(np.float32),
        tw_sin.astype(np.float32),
    )


def dot(a, b):
    return jnp.dot(a, b, preferred_element_type=f32)


def forward(rows, first, middle, tw_cos, tw_sin):
    half = rows.shape[0]
    part = dot(first, rows)
    re, im = part[:half], part[half:]
    turned = jnp.concatenate([re * tw_cos + im * tw_sin, im * tw_cos - re * tw_sin], axis=1)
    return dot(turned.astype(bf16), middle)


def convolve(sig, fil, first, middle, last, tw_cos, tw_sin):
    width = sig.shape[1]
    spec = forward(sig, first, middle, tw_cos, tw_sin)
    gain = forward(fil, first, middle, tw_cos, tw_sin)
    sr, si, gr, gi = spec[:, :width], spec[:, width:], gain[:, :width], gain[:, width:]
    prod = jnp.concatenate([sr * gi + si * gr, sr * gr - si * gi], axis=1).astype(bf16)
    back = dot(prod, middle)
    im, re = back[:, :width], back[:, width:]
    turned = jnp.concatenate([re * tw_cos - im * tw_sin, re * tw_sin + im * tw_cos], axis=0)
    return dot(last, turned.astype(bf16))


def from_behind(array, axis, by):
    devices = lax.axis_size(axis)
    pairs = [(i, i + by) for i in range(devices) if 0 <= i + by < devices]
    return lax.ppermute(array, axis, pairs)


def local(tokens, norm_gain, w_in, short_filter, long_filter, medium_filter, skip_gain, w_out):
    tok_rows, chan_width = tokens.shape
    devices = lax.axis_size("seq")
    my_index = lax.axis_index("seq")
    chans = chan_width // devices
    consts = [jnp.asarray(t) for t in tables(devices, tok_rows, chans)]
    med = jnp.pad(medium_filter, ((0, tok_rows - medium_filter.shape[0]), (0, 0)))
    med = med.at[0].add(skip_gain)
    taps = (long_filter + jnp.where(my_index == 0, med, 0.0)).astype(bf16)
    inputs = tokens.astype(f32)
    mean_sq = jnp.mean(inputs * inputs, axis=-1, keepdims=True)
    normed = (inputs * lax.rsqrt(mean_sq + epsilon) * norm_gain).astype(bf16)
    projected = dot(normed, w_in).astype(bf16)
    taps_count = short_filter.shape[0]
    rim_rows = from_behind(projected[tok_rows - (taps_count - 1) :], "seq", 1)
    extended = jnp.concatenate([rim_rows, projected], axis=0)
    short_mix = jnp.zeros((tok_rows, projected.shape[1]), f32)
    for tap_num in range(taps_count):
        begin = taps_count - 1 - tap_num
        short_mix = short_mix + short_filter[tap_num] * extended[begin : begin + tok_rows]
    query_part = short_mix[:, 0:chan_width]
    signal = short_mix[:, chan_width : 2 * chan_width] * short_mix[:, 2 * chan_width :]

    def spread(array):
        split = array.astype(bf16).T.reshape(devices, chans, tok_rows)
        return lax.all_to_all(split, "seq", 0, 0, tiled=True).reshape(chan_width, tok_rows)

    mixed = convolve(spread(signal), spread(taps), *consts)
    back = spread_back(mixed, devices, chans)
    mixed_out = (query_part * back.T.astype(f32)).astype(bf16)
    return dot(mixed_out, w_out).astype(bf16)


def spread_back(mixed, devices, chans):
    split = mixed.astype(bf16).reshape(devices, chans, mixed.shape[1])
    return lax.all_to_all(split, "seq", 0, 0, tiled=True).reshape(mixed.shape)


def rms_normed(rows, gain):
    rows = rows.astype(f32)
    mean_sq = jnp.mean(rows * rows, axis=-1, keepdims=True)
    return (rows * lax.rsqrt(mean_sq + epsilon) * gain).astype(bf16)


def relative(own, count):
    steps = []
    bit = 1
    while bit < count:
        steps.append((bit, bit * (1 - 2 * (own // bit % 2))))
        bit *= 2
    return [own + sum(step for bit, step in steps if off // bit % 2) for off in range(count - 1, -1, -1)]


def kernel(
    devices,
    tokens_hbm,
    gain_hbm,
    w_in_hbm,
    short_hbm,
    long_hbm,
    med_hbm,
    skip_hbm,
    w_out_hbm,
    all_first_hbm,
    all_turns_hbm,
    all_last_hbm,
    front_first_hbm,
    front_turns_hbm,
    front_last_hbm,
    middle_hbm,
    out_ref,
    tokens,
    gain_ref,
    w_in,
    short_ref,
    long_taps,
    med,
    skip_ref,
    w_out,
    all_first,
    all_turns,
    all_last,
    front_first,
    front_turns,
    front_last,
    middle,
    halo,
    extended,
    signal,
    later,
    sends,
    from_front,
    from_back,
    front_out,
    back_out,
    results,
    ready,
    local_sem,
    halo_sem,
    send_sem,
    recv_sem,
):
    me = lax.axis_index("seq")
    rows, width = tokens.shape
    side = devices // 2
    chans = width // devices
    half = width // 2
    lanes = rows // 2
    fine = chans // 2
    in_front = me < side
    own = lax.rem(me, side)
    cross = relative(own, side)
    same = cross[:-1]
    plane = side // 2
    near = relative(lax.rem(own, plane), plane)
    far = [plane + x for x in near]
    rim = halo.shape[0]
    in_back = jnp.logical_not(in_front)
    barrier = pltpu.get_barrier_semaphore()

    def announce(semaphore, peer):
        pl.semaphore_signal(
            semaphore, inc=1, device_id={"seq": peer}, device_id_type=pl.DeviceIdType.MESH
        )

    @pl.when(in_front)
    def _():
        for d in same:
            announce(barrier, d)
        for d in cross:
            announce(barrier, side + d)

    @pl.when(in_back)
    def _():
        for d in same:
            announce(barrier, side + d)

    loads = [
        pltpu.make_async_copy(source, target, local_sem.at[num])
        for num, (source, target) in enumerate(
            [
                (long_hbm, long_taps),
                (med_hbm, med),
                (skip_hbm, skip_ref),
                (tokens_hbm, tokens),
                (gain_hbm, gain_ref),
                (w_in_hbm, w_in),
                (short_hbm, short_ref),
                (middle_hbm, middle),
                (front_first_hbm, front_first),
                (front_turns_hbm, front_turns),
                (front_last_hbm, front_last),
                (all_first_hbm, all_first),
                (all_turns_hbm, all_turns),
                (all_last_hbm, all_last),
                (w_out_hbm, w_out),
            ]
        )
    ]
    for load in loads[:7]:
        load.start()

    @pl.when(me == devices - 1)
    def _():
        pl.semaphore_wait(barrier, devices - 1)
        for d in cross:
            announce(ready, d)

    def remote(source, target, peer, sent, received):
        return pltpu.make_async_remote_copy(
            src_ref=source,
            dst_ref=target,
            send_sem=send_sem.at[sent],
            recv_sem=recv_sem.at[received],
            device_id={"seq": peer},
            device_id_type=pl.DeviceIdType.MESH,
        )

    def received(ref, num):
        remote(ref, ref, 0, num, num).wait_recv()

    def sent(ref, num):
        remote(ref, ref, 0, num, num).wait_send()

    def same_from_front(kind):
        for d in same:
            remote(sends.at[kind, :, d], from_front.at[kind, own], d, 2 * kind, 2 * kind).start()
        from_front[kind, own] = sends[kind, :, own]

    def cross_from_front(kind):
        for d in cross:
            target = from_front.at[kind, own, 1]
            remote(sends.at[kind, 1, d], target, side + d, 2 * kind + 1, 2 * kind).start()

    def same_from_back(kind):
        for d in same:
            target = from_back.at[kind, own]
            remote(sends.at[kind, 1, d], target, side + d, 2 * kind + 1, 2 * kind + 1).start()
        from_back[kind, own] = sends[kind, 1, own]

    def cross_from_back(kind):
        for d in cross:
            target = from_back.at[kind, own]
            remote(sends.at[kind, 0, d], target, d, 2 * kind, 2 * kind + 1).start()

    def project(part_normed, begin):
        return dot(part_normed, w_in[:, begin:]).astype(bf16).astype(f32)

    def mix(part, begin, count):
        cols = pl.ds(part * width, width)
        total = short_ref[0:1, cols] * extended[rim + begin : rim + begin + count, cols]
        for tap in range(1, short_ref.shape[0]):
            start = rim + begin - tap
            total = total + short_ref[tap : tap + 1, cols] * extended[start : start + count, cols]
        return total

    def turn(ref, begin):
        block = ref[begin : begin + lanes, :].T.reshape(2, side, 2, fine, lanes)
        return jnp.concatenate([block[:, :, 0], block[:, :, 1]], axis=3)

    halo_copy = pltpu.make_async_remote_copy(
        src_ref=tokens.at[pl.ds(rows - rim, rim)],
        dst_ref=halo,
        send_sem=halo_sem.at[0],
        recv_sem=halo_sem.at[1],
        device_id={"seq": lax.rem(me + 1, devices)},
        device_id_type=pl.DeviceIdType.MESH,
    )
    for load in loads[:3]:
        load.wait()

    @pl.when(me == 0)
    def _():
        long_taps[0 : med.shape[0], :] += med[...]
        long_taps[0:1, :] += skip_ref[...]

    sends[0] = jnp.concatenate([turn(long_taps, 0), turn(long_taps, lanes)], axis=2).astype(bf16)
    loads[3].wait()

    @pl.when(in_back)
    def _():
        @pl.when(me < devices - 1)
        def _():
            pl.semaphore_wait(barrier, devices - 1)
            halo_copy.start()

        same_from_back(0)
        cross_from_back(0)

    for load in loads[7:]:
        load.start()
    for load in loads[4:7]:
        load.wait()
    normed = rms_normed(tokens[...], gain_ref[...])
    extended[rim:, width:] = project(normed, width)
    extended[0:rim, :] = jnp.zeros((rim, 3 * width), f32)
    signal[...] = mix(1, 0, rows) * mix(2, 0, rows)
    later[...] = turn(signal, lanes)

    @pl.when(in_front)
    def _():
        pl.semaphore_wait(barrier, side - 1)

        @pl.when(me < side - 1)
        def _():
            halo_copy.start()

        same_from_front(0)

    @pl.when(me > 0)
    def _():
        halo_copy.wait_recv()
        extended[0:rim, :] = project(rms_normed(halo[...], gain_ref[...]), 0)
        signal[0:rim, :] = mix(1, 0, rim) * mix(2, 0, rim)

    sends[1] = jnp.concatenate([turn(signal, 0), later[...]], axis=2).astype(bf16)

    @pl.when(in_front)
    def _():
        same_from_front(1)
        pl.semaphore_wait(ready, 1)

        @pl.when(me == side - 1)
        def _():
            halo_copy.start()

        cross_from_front(0)
        cross_from_front(1)

    @pl.when(in_back)
    def _():
        same_from_back(1)
        cross_from_back(1)

    extended[rim:, :width] = dot(normed, w_in[:, :width]).astype(bf16).astype(f32)
    query = mix(0, 0, rows).T
    for load in loads[7:]:
        load.wait()

    def stacked(left, right):
        pieces = [(left[:, :lanes], right[:, :lanes]), (left[:, lanes:], right[:, lanes:])]
        return jnp.concatenate([jnp.concatenate(pair, axis=1) for pair in pieces], axis=0)

    def spread(array):
        return jnp.concatenate([array[:width], array[width:]], axis=1)

    def spectrum(block, first, turns):
        part = dot(first[...], block)
        re, im = part[:width], part[width:]
        cos_t, sin_t = turns[:width], turns[width:]
        turned = stacked(re * cos_t + im * sin_t, im * cos_t - re * sin_t)
        spec = dot(turned.astype(bf16), middle[...])
        return spec[:, :lanes], spec[:, lanes:]

    def inverse(sig, gain, turns, last):
        (sr, si), (gr, gi) = sig, gain
        prod = jnp.concatenate([sr * gi + si * gr, sr * gr - si * gi], axis=1)
        back = dot(prod.astype(bf16), middle[...])
        im, re = spread(back[:, :lanes]), spread(back[:, lanes:])
        cos_t, sin_t = turns[:width], turns[width:]
        turned = jnp.concatenate([re * cos_t - im * sin_t, re * sin_t + im * cos_t], axis=0)
        return dot(last[...], turned.astype(bf16)).astype(bf16)

    def joined(kind, which):
        front = from_front[kind, :, which].reshape(half, rows)
        return jnp.concatenate([front, from_back[kind].reshape(half, rows)], axis=0)

    def finish():
        mixed = results[...].astype(f32)
        early, late = mixed[:, :, :fine], mixed[:, :, fine:]
        sides = [
            jnp.concatenate([early[:, :, :, cut], late[:, :, :, cut]], axis=3)
            for cut in (slice(0, lanes), slice(lanes, rows))
        ]
        mixed = jnp.concatenate(sides, axis=2).reshape(width, rows)
        gated = (query * mixed).astype(bf16).T
        out_ref[...] = dot(gated, w_out[...]).astype(bf16)

    @pl.when(in_front)
    def _():
        received(from_front.at[0, pl.ds(0, side - 1)], 0)
        gain = spectrum(from_front[0].reshape(width, rows), front_first, front_turns)
        received(from_front.at[1, pl.ds(0, side - 1)], 2)
        sig = spectrum(from_front[1].reshape(width, rows), front_first, front_turns)
        front_out[...] = inverse(sig, gain, front_turns, front_last).reshape(front_out.shape)
        for d in same:
            remote(front_out.at[d], results.at[:, own], d, 4, 4).start()
        results[:, own] = front_out[own]
        received(from_back.at[0], 1)
        back_gain = spectrum(joined(0, 0), all_first, all_turns)
        received(from_back.at[1], 3)
        sig = spectrum(joined(1, 0), all_first, all_turns)
        back_out[...] = inverse(sig, back_gain, all_turns, all_last).reshape(back_out.shape)
        for d in [0, 1, 4, 5, 2, 3, 6, 7]:
            remote(back_out.at[d], results.at[0, own], side + d, 5, 4).start()
        received(results.at[:, pl.ds(0, side - 1)], 4)
        finish()
        for kind in range(2):
            sent(sends.at[kind, :, pl.ds(0, side - 1)], 2 * kind)
            sent(sends.at[kind, 1], 2 * kind + 1)
        sent(front_out.at[pl.ds(0, side - 1)], 4)
        sent(back_out, 5)

    @pl.when(jnp.logical_not(in_front))
    def _():
        received(from_front.at[0, :, 1], 0)
        received(from_back.at[0, pl.ds(0, side - 1)], 1)
        gain = spectrum(joined(0, 1), all_first, all_turns)
        received(from_front.at[1, :, 1], 2)
        received(from_back.at[1, pl.ds(0, side - 1)], 3)
        sig = spectrum(joined(1, 1), all_first, all_turns)
        back_out[...] = inverse(sig, gain, all_turns, all_last).reshape(back_out.shape)
        for d in same:
            remote(back_out.at[d], results.at[1, own], side + d, 5, 5).start()
        results[1, own] = back_out[own]
        received(results.at[0], 4)
        received(results.at[1, pl.ds(0, side - 1)], 5)
        finish()
        for kind in range(2):
            sent(sends.at[kind, 0], 2 * kind)
            sent(sends.at[kind, 1, pl.ds(0, side - 1)], 2 * kind + 1)
        sent(back_out.at[pl.ds(0, side - 1)], 5)

    @pl.when(me < devices - 1)
    def _():
        halo_copy.wait_send()


def fused(tokens, norm_gain, w_in, short_filter, long_filter, medium_filter, skip_gain, w_out):
    rows, width = tokens.shape
    devices = lax.axis_size("seq")
    side = devices // 2
    chans = width // devices
    lanes, fine = rows // 2, chans // 2
    all_first, middle, all_last, *all_turns = tables(2 * devices, lanes, fine)
    front_first, _, front_last, *front_turns = tables(devices, lanes, chans)
    order = np.arange(width).reshape(side, 2, 2, fine).transpose(0, 2, 1, 3).reshape(-1)
    consts = [
        all_first,
        np.tile(np.concatenate(all_turns, axis=0), (1, 2)),
        all_last[width // 2 :],
        front_first[:, order],
        np.tile(np.concatenate(front_turns, axis=0), (1, 2)),
        front_last[order],
        middle,
    ]
    rim = 16
    held = [
        tokens,
        norm_gain.reshape(1, width),
        w_in,
        short_filter,
        long_filter,
        medium_filter,
        skip_gain.reshape(1, width),
        w_out,
        *[jnp.asarray(t) for t in consts],
    ]
    return pl.pallas_call(
        functools.partial(kernel, devices),
        out_shape=pltpu.VMEM((rows, width), bf16),
        in_specs=[pl.BlockSpec(memory_space=pl.ANY)] * len(held),
        out_specs=pl.BlockSpec(memory_space=pltpu.VMEM),
        scratch_shapes=[pltpu.VMEM(a.shape, a.dtype) for a in held]
        + [
            pltpu.VMEM((rim, width), bf16),
            pltpu.VMEM((rim + rows, 3 * width), f32),
            pltpu.VMEM((rows, width), f32),
            pltpu.VMEM((2, side, fine, rows), f32),
            pltpu.VMEM((2, 2, side, chans, rows), bf16),
            pltpu.VMEM((2, side, 2, chans, rows), bf16),
            pltpu.VMEM((2, side, chans, rows), bf16),
            pltpu.VMEM((side, 2, chans, rows), bf16),
            pltpu.VMEM((side, chans, rows), bf16),
            pltpu.VMEM((2, side, chans, rows), bf16),
            pltpu.SemaphoreType.REGULAR,
            pltpu.SemaphoreType.DMA((len(held),)),
            pltpu.SemaphoreType.DMA((2,)),
            pltpu.SemaphoreType.DMA((6,)),
            pltpu.SemaphoreType.DMA((6,)),
        ],
        compiler_params=pltpu.CompilerParams(collective_id=0, has_side_effects=True),
    )(*held)


def solution(mesh):
    placed = (P(("groups", "seq"), None), P(), P(), P(), P("seq", None), P(), P(), P())

    def step(tokens, norm_gain, w_in, short_filter, long_filter, medium_filter, skip_gain, w_out):
        chans = tokens.shape[1] // mesh.shape["seq"]
        whole_tiles = chans == 16 and tokens.shape[0] == tokens.shape[1]
        body = fused if whole_tiles else local
        return body(tokens, norm_gain, w_in, short_filter, long_filter, medium_filter, skip_gain, w_out)

    return jax.shard_map(
        step, mesh=mesh, in_specs=placed, out_specs=P(("groups", "seq"), None), check_vma=False
    )
```

```python
import functools
import math

import jax
import jax.numpy as jnp
import numpy as np
from jax import lax
from jax.experimental import pallas as pl
from jax.experimental.pallas import tpu as pltpu
from jax.sharding import PartitionSpec as P

epsilon = 1e-06
bf16 = jnp.bfloat16
f32 = jnp.float32


def tables(devices, tok_rows, chans):
    full = devices * tok_rows
    idx = np.arange(devices)
    angle = 2.0 * math.pi * ((idx[:, None] * (4 * idx[None, :] + 1)) % (4 * devices)) / (4 * devices)
    eye = np.eye(chans)
    outer_cos = np.kron(np.cos(angle), eye)
    outer_sin = np.kron(np.sin(angle), eye)
    first = np.concatenate([outer_cos.T, -outer_sin.T], axis=0)
    last = np.concatenate([outer_cos, -outer_sin], axis=1) / full
    pos = np.arange(tok_rows)
    turn = 2.0 * math.pi * ((4 * idx[:, None] + 1) * pos[None, :]) / (4 * full)
    tw_cos = np.repeat(np.cos(turn), chans, axis=0)
    tw_sin = np.repeat(np.sin(turn), chans, axis=0)
    inner = 2.0 * math.pi * (pos[:, None] * pos[None, :] % tok_rows) / tok_rows
    cos_t, sin_t = np.cos(inner), np.sin(inner)
    middle = np.block([[cos_t, -sin_t], [sin_t, cos_t]])
    return (
        first.astype(bf16),
        middle.astype(bf16),
        last.astype(bf16),
        tw_cos.astype(np.float32),
        tw_sin.astype(np.float32),
    )


def dot(a, b):
    return jnp.dot(a, b, preferred_element_type=f32)


def forward(rows, first, middle, tw_cos, tw_sin):
    half = rows.shape[0]
    part = dot(first, rows)
    re, im = part[:half], part[half:]
    turned = jnp.concatenate([re * tw_cos + im * tw_sin, im * tw_cos - re * tw_sin], axis=1)
    return dot(turned.astype(bf16), middle)


def convolve(sig, fil, first, middle, last, tw_cos, tw_sin):
    width = sig.shape[1]
    spec = forward(sig, first, middle, tw_cos, tw_sin)
    gain = forward(fil, first, middle, tw_cos, tw_sin)
    sr, si, gr, gi = spec[:, :width], spec[:, width:], gain[:, :width], gain[:, width:]
    prod = jnp.concatenate([sr * gi + si * gr, sr * gr - si * gi], axis=1).astype(bf16)
    back = dot(prod, middle)
    im, re = back[:, :width], back[:, width:]
    turned = jnp.concatenate([re * tw_cos - im * tw_sin, re * tw_sin + im * tw_cos], axis=0)
    return dot(last, turned.astype(bf16))


def from_behind(array, axis, by):
    devices = lax.axis_size(axis)
    pairs = [(i, i + by) for i in range(devices) if 0 <= i + by < devices]
    return lax.ppermute(array, axis, pairs)


def local(tokens, norm_gain, w_in, short_filter, long_filter, medium_filter, skip_gain, w_out):
    tok_rows, chan_width = tokens.shape
    devices = lax.axis_size("seq")
    my_index = lax.axis_index("seq")
    chans = chan_width // devices
    consts = [jnp.asarray(t) for t in tables(devices, tok_rows, chans)]
    med = jnp.pad(medium_filter, ((0, tok_rows - medium_filter.shape[0]), (0, 0)))
    med = med.at[0].add(skip_gain)
    taps = (long_filter + jnp.where(my_index == 0, med, 0.0)).astype(bf16)
    inputs = tokens.astype(f32)
    mean_sq = jnp.mean(inputs * inputs, axis=-1, keepdims=True)
    normed = (inputs * lax.rsqrt(mean_sq + epsilon) * norm_gain).astype(bf16)
    projected = dot(normed, w_in).astype(bf16)
    taps_count = short_filter.shape[0]
    rim_rows = from_behind(projected[tok_rows - (taps_count - 1) :], "seq", 1)
    extended = jnp.concatenate([rim_rows, projected], axis=0)
    short_mix = jnp.zeros((tok_rows, projected.shape[1]), f32)
    for tap_num in range(taps_count):
        begin = taps_count - 1 - tap_num
        short_mix = short_mix + short_filter[tap_num] * extended[begin : begin + tok_rows]
    query_part = short_mix[:, 0:chan_width]
    signal = short_mix[:, chan_width : 2 * chan_width] * short_mix[:, 2 * chan_width :]

    def spread(array):
        split = array.astype(bf16).T.reshape(devices, chans, tok_rows)
        return lax.all_to_all(split, "seq", 0, 0, tiled=True).reshape(chan_width, tok_rows)

    mixed = convolve(spread(signal), spread(taps), *consts)
    back = spread_back(mixed, devices, chans)
    mixed_out = (query_part * back.T.astype(f32)).astype(bf16)
    return dot(mixed_out, w_out).astype(bf16)


def spread_back(mixed, devices, chans):
    split = mixed.astype(bf16).reshape(devices, chans, mixed.shape[1])
    return lax.all_to_all(split, "seq", 0, 0, tiled=True).reshape(mixed.shape)


def rms_normed(rows, gain):
    rows = rows.astype(f32)
    mean_sq = jnp.mean(rows * rows, axis=-1, keepdims=True)
    return (rows * lax.rsqrt(mean_sq + epsilon) * gain).astype(bf16)


def relative(own, count):
    steps = []
    bit = 1
    while bit < count:
        steps.append((bit, bit * (1 - 2 * (own // bit % 2))))
        bit *= 2
    return [own + sum(step for bit, step in steps if off // bit % 2) for off in range(count - 1, -1, -1)]


def kernel(
    devices,
    tokens_hbm,
    gain_hbm,
    w_in_hbm,
    short_hbm,
    long_hbm,
    med_hbm,
    skip_hbm,
    w_out_hbm,
    matrices_hbm,
    turns_hbm,
    out_ref,
    tokens,
    gain_ref,
    w_in,
    short_ref,
    long_taps,
    med,
    skip_ref,
    w_out,
    matrices,
    turns,
    halo,
    extended,
    signal,
    later,
    sends,
    from_front,
    from_back,
    front_out,
    back_out,
    results,
    ready,
    local_sem,
    halo_sem,
    send_sem,
    recv_sem,
):
    me = lax.axis_index("seq")
    rows, width = tokens.shape
    side = devices // 2
    chans = width // devices
    half = width // 2
    lanes = rows // 2
    fine = chans // 2
    in_front = me < side
    own = lax.rem(me, side)
    cross = relative(own, side)
    same = cross[:-1]
    plane = side // 2
    near = relative(lax.rem(own, plane), plane)
    far = [plane + x for x in near]
    rim = halo.shape[0]
    in_back = jnp.logical_not(in_front)
    barrier = pltpu.get_barrier_semaphore()

    def announce(semaphore, peer):
        pl.semaphore_signal(
            semaphore, inc=1, device_id={"seq": peer}, device_id_type=pl.DeviceIdType.MESH
        )

    @pl.when(in_front)
    def _():
        for d in same:
            announce(barrier, d)
        for d in cross:
            announce(barrier, side + d)

    @pl.when(in_back)
    def _():
        for d in same:
            announce(barrier, side + d)

    def copies(pairs):
        return [
            pltpu.make_async_copy(source, target, local_sem.at[num])
            for num, (source, target) in enumerate(pairs)
        ]

    loads = copies(
        [
            (long_hbm, long_taps),
            (tokens_hbm, tokens),
            (gain_hbm, gain_ref),
            (w_in_hbm, w_in),
            (short_hbm, short_ref),
        ]
    )
    later_loads = copies([(matrices_hbm, matrices), (w_out_hbm, w_out), (turns_hbm, turns)])
    for load in loads:
        load.start()

    @pl.when(me == devices - 1)
    def _():
        pl.semaphore_wait(barrier, devices - 1)
        for d in cross:
            announce(ready, d)

    def remote(source, target, peer, sent, received):
        return pltpu.make_async_remote_copy(
            src_ref=source,
            dst_ref=target,
            send_sem=send_sem.at[sent],
            recv_sem=recv_sem.at[received],
            device_id={"seq": peer},
            device_id_type=pl.DeviceIdType.MESH,
        )

    def received(ref, num):
        remote(ref, ref, 0, num, num).wait_recv()

    def sent(ref, num):
        remote(ref, ref, 0, num, num).wait_send()

    def same_from_front(kind):
        for d in same:
            remote(sends.at[kind, :, d], from_front.at[kind, own], d, 0, 2 * kind).start()
        from_front[kind, own] = sends[kind, :, own]

    def cross_from_front(kind):
        for d in cross:
            target = from_front.at[kind, own, 1]
            remote(sends.at[kind, 1, d], target, side + d, 1, 2 * kind).start()

    def same_from_back(kind):
        for d in same:
            target = from_back.at[kind, own]
            remote(sends.at[kind, 1, d], target, side + d, 1, 2 * kind + 1).start()
        from_back[kind, own] = sends[kind, 1, own]

    def cross_from_back(kind):
        for d in cross:
            target = from_back.at[kind, own]
            remote(sends.at[kind, 0, d], target, d, 0, 2 * kind + 1).start()

    def project(part_normed, begin):
        return dot(part_normed, w_in[:, begin:]).astype(bf16).astype(f32)

    def mix(part, begin, count):
        cols = pl.ds(part * width, width)
        total = short_ref[0:1, cols] * extended[rim + begin : rim + begin + count, cols]
        for tap in range(1, short_ref.shape[0]):
            start = rim + begin - tap
            total = total + short_ref[tap : tap + 1, cols] * extended[start : start + count, cols]
        return total

    def turn(ref, begin):
        block = ref[begin : begin + lanes, :].T.reshape(2, side, 2, fine, lanes)
        return jnp.concatenate([block[:, :, 0], block[:, :, 1]], axis=3)

    halo_copy = pltpu.make_async_remote_copy(
        src_ref=tokens.at[pl.ds(rows - rim, rim)],
        dst_ref=halo,
        send_sem=halo_sem.at[0],
        recv_sem=halo_sem.at[1],
        device_id={"seq": lax.rem(me + 1, devices)},
        device_id_type=pl.DeviceIdType.MESH,
    )
    loads[0].wait()

    @pl.when(me == 0)
    def _():
        for load in copies([(med_hbm, med)]):
            load.start()
            load.wait()
        for load in copies([(skip_hbm, skip_ref)]):
            load.start()
            load.wait()
        long_taps[0 : med.shape[0], :] += med[...]
        long_taps[0:1, :] += skip_ref[...]

    sends[0] = jnp.concatenate([turn(long_taps, 0), turn(long_taps, lanes)], axis=2).astype(bf16)
    loads[1].wait()

    @pl.when(in_back)
    def _():
        @pl.when(me < devices - 1)
        def _():
            pl.semaphore_wait(barrier, devices - 1)
            halo_copy.start()

        same_from_back(0)
        cross_from_back(0)

    for load in loads[2:]:
        load.wait()
    for load in later_loads:
        load.start()
    normed = rms_normed(tokens[...], gain_ref[...])
    extended[rim:, width:] = project(normed, width)
    extended[0:rim, :] = jnp.zeros((rim, 3 * width), f32)
    signal[...] = mix(1, 0, rows) * mix(2, 0, rows)
    later[...] = turn(signal, lanes)

    @pl.when(in_front)
    def _():
        pl.semaphore_wait(barrier, side - 1)

        @pl.when(me < side - 1)
        def _():
            halo_copy.start()

        same_from_front(0)

    @pl.when(me > 0)
    def _():
        halo_copy.wait_recv()
        extended[0:rim, :] = project(rms_normed(halo[...], gain_ref[...]), 0)
        signal[0:rim, :] = mix(1, 0, rim) * mix(2, 0, rim)

    sends[1] = jnp.concatenate([turn(signal, 0), later[...]], axis=2).astype(bf16)

    @pl.when(in_front)
    def _():
        same_from_front(1)
        pl.semaphore_wait(ready, 1)

        @pl.when(me == side - 1)
        def _():
            halo_copy.start()

        cross_from_front(0)
        cross_from_front(1)

    @pl.when(in_back)
    def _():
        same_from_back(1)
        cross_from_back(1)

    extended[rim:, :width] = dot(normed, w_in[:, :width]).astype(bf16).astype(f32)
    query = mix(0, 0, rows).T
    for load in later_loads:
        load.wait()
    sizes = [2 * width, 2 * width, width, 2 * width, width]
    begins = [sum(sizes[:num]) for num in range(len(sizes))]
    views = [matrices.at[pl.ds(begin, size)] for begin, size in zip(begins, sizes)]
    all_first, front_first, middle, front_last, all_last = views
    all_turns, front_turns = (turns.at[pl.ds(side_begin, 2 * width)] for side_begin in (0, 2 * width))

    def stacked(left, right):
        pieces = [(left[:, :lanes], right[:, :lanes]), (left[:, lanes:], right[:, lanes:])]
        return jnp.concatenate([jnp.concatenate(pair, axis=1) for pair in pieces], axis=0)

    def spread(array):
        return jnp.concatenate([array[:width], array[width:]], axis=1)

    def spectrum(block, first, turns):
        part = dot(first[...], block)
        re, im = part[:width], part[width:]
        cos_t, sin_t = turns[:width], turns[width:]
        turned = stacked(re * cos_t + im * sin_t, im * cos_t - re * sin_t)
        spec = dot(turned.astype(bf16), middle[...])
        return spec[:, :lanes], spec[:, lanes:]

    def inverse(sig, gain, turns, last):
        (sr, si), (gr, gi) = sig, gain
        prod = jnp.concatenate([sr * gi + si * gr, sr * gr - si * gi], axis=1)
        back = dot(prod.astype(bf16), middle[...])
        im, re = spread(back[:, :lanes]), spread(back[:, lanes:])
        cos_t, sin_t = turns[:width], turns[width:]
        left, right = re * cos_t - im * sin_t, re * sin_t + im * cos_t
        count = last.shape[0] // 2
        total = dot(last[:count], left.astype(bf16)) + dot(last[count:], right.astype(bf16))
        return total.astype(bf16)

    def joined(kind, which):
        front = from_front[kind, :, which].reshape(half, rows)
        return jnp.concatenate([front, from_back[kind].reshape(half, rows)], axis=0)

    def finish():
        mixed = results[...].astype(f32)
        early, late = mixed[:, :, :fine], mixed[:, :, fine:]
        sides = [
            jnp.concatenate([early[:, :, :, cut], late[:, :, :, cut]], axis=3)
            for cut in (slice(0, lanes), slice(lanes, rows))
        ]
        mixed = jnp.concatenate(sides, axis=2).reshape(width, rows)
        gated = (query * mixed).astype(bf16).T
        out_ref[...] = dot(gated, w_out[...]).astype(bf16)

    @pl.when(in_front)
    def _():
        received(from_front.at[0, pl.ds(0, side - 1)], 0)
        gain = spectrum(from_front[0].reshape(width, rows), front_first, front_turns)
        received(from_front.at[1, pl.ds(0, side - 1)], 2)
        sig = spectrum(from_front[1].reshape(width, rows), front_first, front_turns)
        front_out[...] = inverse(sig, gain, front_turns, front_last).reshape(front_out.shape)
        for d in same:
            remote(front_out.at[d], results.at[:, own], d, 2, 4).start()
        results[:, own] = front_out[own]
        received(from_back.at[0], 1)
        back_gain = spectrum(joined(0, 0), all_first, all_turns)
        received(from_back.at[1], 3)
        sig = spectrum(joined(1, 0), all_first, all_turns)
        back_out[...] = inverse(sig, back_gain, all_turns, all_last).reshape(back_out.shape)
        for d in [0, 1, 4, 5, 2, 3, 6, 7]:
            remote(back_out.at[d], results.at[0, own], side + d, 3, 4).start()
        received(results.at[:, pl.ds(0, side - 1)], 4)
        finish()
        sent(sends.at[:, :, pl.ds(0, side - 1)], 0)
        sent(sends.at[:, 1], 1)
        sent(front_out.at[pl.ds(0, side - 1)], 2)
        sent(back_out, 3)

    @pl.when(jnp.logical_not(in_front))
    def _():
        received(from_front.at[0, :, 1], 0)
        received(from_back.at[0, pl.ds(0, side - 1)], 1)
        gain = spectrum(joined(0, 1), all_first, all_turns)
        received(from_front.at[1, :, 1], 2)
        received(from_back.at[1, pl.ds(0, side - 1)], 3)
        sig = spectrum(joined(1, 1), all_first, all_turns)
        back_out[...] = inverse(sig, gain, all_turns, all_last).reshape(back_out.shape)
        for d in same:
            remote(back_out.at[d], results.at[1, own], side + d, 3, 5).start()
        results[1, own] = back_out[own]
        received(results.at[0], 4)
        received(results.at[1, pl.ds(0, side - 1)], 5)
        finish()
        sent(sends.at[:, 0], 0)
        sent(sends.at[:, 1, pl.ds(0, side - 1)], 1)
        sent(back_out.at[pl.ds(0, side - 1)], 3)

    @pl.when(me < devices - 1)
    def _():
        halo_copy.wait_send()


def fused(tokens, norm_gain, w_in, short_filter, long_filter, medium_filter, skip_gain, w_out):
    rows, width = tokens.shape
    devices = lax.axis_size("seq")
    side = devices // 2
    chans = width // devices
    lanes, fine = rows // 2, chans // 2
    all_first, middle, all_last, *all_turns = tables(2 * devices, lanes, fine)
    front_first, _, front_last, *front_turns = tables(devices, lanes, chans)
    order = np.arange(width).reshape(side, 2, 2, fine).transpose(0, 2, 1, 3).reshape(-1)

    def split(matrix):
        return np.concatenate([matrix[:, :width], matrix[:, width:]], axis=0)

    matrices = [
        all_first,
        front_first[:, order],
        middle,
        split(front_last[order]),
        split(all_last[width // 2 :]),
    ]
    consts = [
        np.concatenate(matrices, axis=0),
        np.tile(np.concatenate([*all_turns, *front_turns], axis=0), (1, 2)),
    ]
    rim = 16
    held = [
        tokens,
        norm_gain.reshape(1, width),
        w_in,
        short_filter,
        long_filter,
        medium_filter,
        skip_gain.reshape(1, width),
        w_out,
        *[jnp.asarray(t) for t in consts],
    ]
    return pl.pallas_call(
        functools.partial(kernel, devices),
        out_shape=pltpu.VMEM((rows, width), bf16),
        in_specs=[pl.BlockSpec(memory_space=pl.ANY)] * len(held),
        out_specs=pl.BlockSpec(memory_space=pltpu.VMEM),
        scratch_shapes=[pltpu.VMEM(a.shape, a.dtype) for a in held]
        + [
            pltpu.VMEM((rim, width), bf16),
            pltpu.VMEM((rim + rows, 3 * width), f32),
            pltpu.VMEM((rows, width), f32),
            pltpu.VMEM((2, side, fine, rows), f32),
            pltpu.VMEM((2, 2, side, chans, rows), bf16),
            pltpu.VMEM((2, side, 2, chans, rows), bf16),
            pltpu.VMEM((2, side, chans, rows), bf16),
            pltpu.VMEM((side, 2, chans, rows), bf16),
            pltpu.VMEM((side, chans, rows), bf16),
            pltpu.VMEM((2, side, chans, rows), bf16),
            pltpu.SemaphoreType.REGULAR,
            pltpu.SemaphoreType.DMA((5,)),
            pltpu.SemaphoreType.DMA((2,)),
            pltpu.SemaphoreType.DMA((4,)),
            pltpu.SemaphoreType.DMA((6,)),
        ],
        compiler_params=pltpu.CompilerParams(collective_id=0, has_side_effects=True),
    )(*held)


def solution(mesh):
    placed = (P(("groups", "seq"), None), P(), P(), P(), P("seq", None), P(), P(), P())

    def step(tokens, norm_gain, w_in, short_filter, long_filter, medium_filter, skip_gain, w_out):
        chans = tokens.shape[1] // mesh.shape["seq"]
        whole_tiles = chans == 16 and tokens.shape[0] == tokens.shape[1]
        body = fused if whole_tiles else local
        return body(tokens, norm_gain, w_in, short_filter, long_filter, medium_filter, skip_gain, w_out)

    return jax.shard_map(
        step, mesh=mesh, in_specs=placed, out_specs=P(("groups", "seq"), None), check_vma=False
    )
```

```python
import functools
import math

import jax
import jax.numpy as jnp
import numpy as np
from jax import lax
from jax.experimental import pallas as pl
from jax.experimental.pallas import tpu as pltpu
from jax.sharding import PartitionSpec as P

epsilon = 1e-06
bf16 = jnp.bfloat16
f32 = jnp.float32


def tables(devices, tok_rows, chans):
    full = devices * tok_rows
    idx = np.arange(devices)
    angle = 2.0 * math.pi * ((idx[:, None] * (4 * idx[None, :] + 1)) % (4 * devices)) / (4 * devices)
    eye = np.eye(chans)
    outer_cos = np.kron(np.cos(angle), eye)
    outer_sin = np.kron(np.sin(angle), eye)
    first = np.concatenate([outer_cos.T, -outer_sin.T], axis=0)
    last = np.concatenate([outer_cos, -outer_sin], axis=1) / full
    pos = np.arange(tok_rows)
    turn = 2.0 * math.pi * ((4 * idx[:, None] + 1) * pos[None, :]) / (4 * full)
    tw_cos = np.repeat(np.cos(turn), chans, axis=0)
    tw_sin = np.repeat(np.sin(turn), chans, axis=0)
    inner = 2.0 * math.pi * (pos[:, None] * pos[None, :] % tok_rows) / tok_rows
    cos_t, sin_t = np.cos(inner), np.sin(inner)
    middle = np.block([[cos_t, -sin_t], [sin_t, cos_t]])
    return (
        first.astype(bf16),
        middle.astype(bf16),
        last.astype(bf16),
        tw_cos.astype(np.float32),
        tw_sin.astype(np.float32),
    )


def dot(a, b):
    return jnp.dot(a, b, preferred_element_type=f32)


def forward(rows, first, middle, tw_cos, tw_sin):
    half = rows.shape[0]
    part = dot(first, rows)
    re, im = part[:half], part[half:]
    turned = jnp.concatenate([re * tw_cos + im * tw_sin, im * tw_cos - re * tw_sin], axis=1)
    return dot(turned.astype(bf16), middle)


def convolve(sig, fil, first, middle, last, tw_cos, tw_sin):
    width = sig.shape[1]
    spec = forward(sig, first, middle, tw_cos, tw_sin)
    gain = forward(fil, first, middle, tw_cos, tw_sin)
    sr, si, gr, gi = spec[:, :width], spec[:, width:], gain[:, :width], gain[:, width:]
    prod = jnp.concatenate([sr * gi + si * gr, sr * gr - si * gi], axis=1).astype(bf16)
    back = dot(prod, middle)
    im, re = back[:, :width], back[:, width:]
    turned = jnp.concatenate([re * tw_cos - im * tw_sin, re * tw_sin + im * tw_cos], axis=0)
    return dot(last, turned.astype(bf16))


def from_behind(array, axis, by):
    devices = lax.axis_size(axis)
    pairs = [(i, i + by) for i in range(devices) if 0 <= i + by < devices]
    return lax.ppermute(array, axis, pairs)


def local(tokens, norm_gain, w_in, short_filter, long_filter, medium_filter, skip_gain, w_out):
    tok_rows, chan_width = tokens.shape
    devices = lax.axis_size("seq")
    my_index = lax.axis_index("seq")
    chans = chan_width // devices
    consts = [jnp.asarray(t) for t in tables(devices, tok_rows, chans)]
    med = jnp.pad(medium_filter, ((0, tok_rows - medium_filter.shape[0]), (0, 0)))
    med = med.at[0].add(skip_gain)
    taps = (long_filter + jnp.where(my_index == 0, med, 0.0)).astype(bf16)
    inputs = tokens.astype(f32)
    mean_sq = jnp.mean(inputs * inputs, axis=-1, keepdims=True)
    normed = (inputs * lax.rsqrt(mean_sq + epsilon) * norm_gain).astype(bf16)
    projected = dot(normed, w_in).astype(bf16)
    taps_count = short_filter.shape[0]
    rim_rows = from_behind(projected[tok_rows - (taps_count - 1) :], "seq", 1)
    extended = jnp.concatenate([rim_rows, projected], axis=0)
    short_mix = jnp.zeros((tok_rows, projected.shape[1]), f32)
    for tap_num in range(taps_count):
        begin = taps_count - 1 - tap_num
        short_mix = short_mix + short_filter[tap_num] * extended[begin : begin + tok_rows]
    query_part = short_mix[:, 0:chan_width]
    signal = short_mix[:, chan_width : 2 * chan_width] * short_mix[:, 2 * chan_width :]

    def spread(array):
        split = array.astype(bf16).T.reshape(devices, chans, tok_rows)
        return lax.all_to_all(split, "seq", 0, 0, tiled=True).reshape(chan_width, tok_rows)

    mixed = convolve(spread(signal), spread(taps), *consts)
    back = spread_back(mixed, devices, chans)
    mixed_out = (query_part * back.T.astype(f32)).astype(bf16)
    return dot(mixed_out, w_out).astype(bf16)


def spread_back(mixed, devices, chans):
    split = mixed.astype(bf16).reshape(devices, chans, mixed.shape[1])
    return lax.all_to_all(split, "seq", 0, 0, tiled=True).reshape(mixed.shape)


def rms_normed(rows, gain):
    rows = rows.astype(f32)
    mean_sq = jnp.mean(rows * rows, axis=-1, keepdims=True)
    return (rows * lax.rsqrt(mean_sq + epsilon) * gain).astype(bf16)


def relative(own, count):
    steps = []
    bit = 1
    while bit < count:
        steps.append((bit, bit * (1 - 2 * (own // bit % 2))))
        bit *= 2
    return [own + sum(step for bit, step in steps if off // bit % 2) for off in range(count - 1, -1, -1)]


def kernel(
    devices,
    tokens_hbm,
    gain_hbm,
    w_in_hbm,
    short_hbm,
    long_hbm,
    med_hbm,
    skip_hbm,
    w_out_hbm,
    matrices_hbm,
    turns_hbm,
    out_ref,
    tokens,
    gain_ref,
    w_in,
    short_ref,
    long_taps,
    med,
    skip_ref,
    w_out,
    matrices,
    turns,
    halo,
    extended,
    signal,
    later,
    sends,
    from_front,
    from_back,
    front_out,
    back_out,
    results,
    ready,
    local_sem,
    halo_sem,
    send_sem,
    recv_sem,
):
    me = lax.axis_index("seq")
    rows, width = tokens.shape
    side = devices // 2
    chans = width // devices
    half = width // 2
    lanes = rows // 2
    fine = chans // 2
    in_front = me < side
    own = lax.rem(me, side)
    cross = relative(own, side)
    same = cross[:-1]
    plane = side // 2
    near = relative(lax.rem(own, plane), plane)
    far = [plane + x for x in near]
    rim = halo.shape[0]
    def copies(pairs):
        return [
            pltpu.make_async_copy(source, target, local_sem.at[num])
            for num, (source, target) in enumerate(pairs)
        ]

    loads = copies(
        [
            (long_hbm, long_taps),
            (tokens_hbm, tokens),
            (gain_hbm, gain_ref),
            (w_in_hbm, w_in),
            (short_hbm, short_ref),
        ]
    )
    later_loads = copies([(matrices_hbm, matrices), (w_out_hbm, w_out), (turns_hbm, turns)])
    for load in loads[:5]:
        load.start()

    in_back = jnp.logical_not(in_front)
    barrier = pltpu.get_barrier_semaphore()

    def announce(semaphore, peer):
        pl.semaphore_signal(
            semaphore, inc=1, device_id={"seq": peer}, device_id_type=pl.DeviceIdType.MESH
        )

    @pl.when(in_front)
    def _():
        for d in same:
            announce(barrier, d)
        for d in cross:
            announce(barrier, side + d)

    @pl.when(in_back)
    def _():
        for d in same[-1:] + same[:-1]:
            announce(barrier, side + d)

    for load in loads[5:]:
        load.start()

    @pl.when(me == devices - 1)
    def _():
        pl.semaphore_wait(barrier, devices - 1)
        for d in cross:
            announce(ready, d)

    def remote(source, target, peer, sent, received):
        return pltpu.make_async_remote_copy(
            src_ref=source,
            dst_ref=target,
            send_sem=send_sem.at[sent],
            recv_sem=recv_sem.at[received],
            device_id={"seq": peer},
            device_id_type=pl.DeviceIdType.MESH,
        )

    def received(ref, num):
        remote(ref, ref, 0, num, num).wait_recv()

    def sent(ref, num):
        remote(ref, ref, 0, num, num).wait_send()

    def same_from_front(kind):
        for d in same:
            remote(sends.at[kind, :, d], from_front.at[kind, own], d, 0, 2 * kind).start()
        from_front[kind, own] = sends[kind, :, own]

    def cross_from_front(kind):
        for d in cross:
            target = from_front.at[kind, own, 1]
            remote(sends.at[kind, 1, d], target, side + d, 1, 2 * kind).start()

    def same_from_back(kind):
        for d in same:
            target = from_back.at[kind, own]
            remote(sends.at[kind, 1, d], target, side + d, 1, 2 * kind + 1).start()
        from_back[kind, own] = sends[kind, 1, own]

    def cross_from_back(kind):
        for d in cross:
            target = from_back.at[kind, own]
            remote(sends.at[kind, 0, d], target, d, 0, 2 * kind + 1).start()

    def project(part_normed, begin):
        return dot(part_normed, w_in[:, begin:]).astype(bf16).astype(f32)

    def mix(part, begin, count):
        cols = pl.ds(part * width, width)
        total = short_ref[0:1, cols] * extended[rim + begin : rim + begin + count, cols]
        for tap in range(1, short_ref.shape[0]):
            start = rim + begin - tap
            total = total + short_ref[tap : tap + 1, cols] * extended[start : start + count, cols]
        return total

    def turn(ref, begin):
        block = ref[begin : begin + lanes, :].T.reshape(2, side, 2, fine, lanes)
        return jnp.concatenate([block[:, :, 0], block[:, :, 1]], axis=3)

    halo_copy = pltpu.make_async_remote_copy(
        src_ref=tokens.at[pl.ds(rows - rim, rim)],
        dst_ref=halo,
        send_sem=halo_sem.at[0],
        recv_sem=halo_sem.at[1],
        device_id={"seq": lax.rem(me + 1, devices)},
        device_id_type=pl.DeviceIdType.MESH,
    )
    loads[0].wait()

    @pl.when(me == 0)
    def _():
        for load in copies([(med_hbm, med)]):
            load.start()
            load.wait()
        for load in copies([(skip_hbm, skip_ref)]):
            load.start()
            load.wait()
        long_taps[0 : med.shape[0], :] += med[...]
        long_taps[0:1, :] += skip_ref[...]

    sends[0] = jnp.concatenate([turn(long_taps, 0), turn(long_taps, lanes)], axis=2).astype(bf16)
    loads[1].wait()

    @pl.when(in_back)
    def _():
        @pl.when(me < devices - 1)
        def _():
            pl.semaphore_wait(barrier, devices - 1)
            halo_copy.start()

        same_from_back(0)
        cross_from_back(0)

    for load in loads[2:]:
        load.wait()
    for load in later_loads:
        load.start()
    normed = rms_normed(tokens[...], gain_ref[...])
    extended[rim:, width:] = project(normed, width)
    extended[0:rim, :] = jnp.zeros((rim, 3 * width), f32)
    signal[...] = mix(1, 0, rows) * mix(2, 0, rows)
    later[...] = turn(signal, lanes)

    @pl.when(in_front)
    def _():
        pl.semaphore_wait(barrier, side - 1)

        @pl.when(me < side - 1)
        def _():
            halo_copy.start()

        same_from_front(0)

    @pl.when(me > 0)
    def _():
        halo_copy.wait_recv()
        extended[0:rim, :] = project(rms_normed(halo[...], gain_ref[...]), 0)
        signal[0:rim, :] = mix(1, 0, rim) * mix(2, 0, rim)

    sends[1] = jnp.concatenate([turn(signal, 0), later[...]], axis=2).astype(bf16)

    @pl.when(in_front)
    def _():
        same_from_front(1)
        pl.semaphore_wait(ready, 1)

        @pl.when(me == side - 1)
        def _():
            halo_copy.start()

        cross_from_front(0)
        cross_from_front(1)

    @pl.when(in_back)
    def _():
        same_from_back(1)
        cross_from_back(1)

    extended[rim:, :width] = dot(normed, w_in[:, :width]).astype(bf16).astype(f32)
    query = mix(0, 0, rows).T
    for load in later_loads:
        load.wait()
    sizes = [2 * width, 2 * width, width, 2 * width, width]
    begins = [sum(sizes[:num]) for num in range(len(sizes))]
    views = [matrices.at[pl.ds(begin, size)] for begin, size in zip(begins, sizes)]
    all_first, front_first, middle, front_last, all_last = views
    all_turns, front_turns = (turns.at[pl.ds(side_begin, 2 * width)] for side_begin in (0, 2 * width))

    def stacked(left, right):
        pieces = [(left[:, :lanes], right[:, :lanes]), (left[:, lanes:], right[:, lanes:])]
        return jnp.concatenate([jnp.concatenate(pair, axis=1) for pair in pieces], axis=0)

    def spread(array):
        return jnp.concatenate([array[:width], array[width:]], axis=1)

    def spectrum(block, first, turns):
        part = dot(first[...], block)
        re, im = part[:width], part[width:]
        cos_t, sin_t = turns[:width], turns[width:]
        turned = stacked(re * cos_t + im * sin_t, im * cos_t - re * sin_t)
        spec = dot(turned.astype(bf16), middle[...])
        return spec[:, :lanes], spec[:, lanes:]

    def inverse(sig, gain, turns, last):
        (sr, si), (gr, gi) = sig, gain
        prod = jnp.concatenate([sr * gi + si * gr, sr * gr - si * gi], axis=1)
        back = dot(prod.astype(bf16), middle[...])
        im, re = spread(back[:, :lanes]), spread(back[:, lanes:])
        cos_t, sin_t = turns[:width], turns[width:]
        left, right = re * cos_t - im * sin_t, re * sin_t + im * cos_t
        count = last.shape[0] // 2
        total = dot(last[:count], left.astype(bf16)) + dot(last[count:], right.astype(bf16))
        return total.astype(bf16)

    def joined(kind, which):
        front = from_front[kind, :, which].reshape(half, rows)
        return jnp.concatenate([front, from_back[kind].reshape(half, rows)], axis=0)

    def finish():
        mixed = results[...].astype(f32)
        early, late = mixed[:, :, :fine], mixed[:, :, fine:]
        sides = [
            jnp.concatenate([early[:, :, :, cut], late[:, :, :, cut]], axis=3)
            for cut in (slice(0, lanes), slice(lanes, rows))
        ]
        mixed = jnp.concatenate(sides, axis=2).reshape(width, rows)
        gated = (query * mixed).astype(bf16).T
        out_ref[...] = dot(gated, w_out[...]).astype(bf16)

    @pl.when(in_front)
    def _():
        received(from_front.at[0, pl.ds(0, side - 1)], 0)
        gain = spectrum(from_front[0].reshape(width, rows), front_first, front_turns)
        received(from_front.at[1, pl.ds(0, side - 1)], 2)
        sig = spectrum(from_front[1].reshape(width, rows), front_first, front_turns)
        front_out[...] = inverse(sig, gain, front_turns, front_last).reshape(front_out.shape)
        for d in same:
            remote(front_out.at[d], results.at[:, own], d, 2, 4).start()
        results[:, own] = front_out[own]
        received(from_back.at[0], 1)
        back_gain = spectrum(joined(0, 0), all_first, all_turns)
        received(from_back.at[1], 3)
        sig = spectrum(joined(1, 0), all_first, all_turns)
        back_out[...] = inverse(sig, back_gain, all_turns, all_last).reshape(back_out.shape)
        for d in [0, 1, 4, 5, 2, 3, 6, 7]:
            remote(back_out.at[d], results.at[0, own], side + d, 3, 4).start()
        received(results.at[:, pl.ds(0, side - 1)], 4)
        finish()
        sent(sends.at[:, :, pl.ds(0, side - 1)], 0)
        sent(sends.at[:, 1], 1)
        sent(front_out.at[pl.ds(0, side - 1)], 2)
        sent(back_out, 3)

    @pl.when(jnp.logical_not(in_front))
    def _():
        received(from_front.at[0, :, 1], 0)
        received(from_back.at[0, pl.ds(0, side - 1)], 1)
        gain = spectrum(joined(0, 1), all_first, all_turns)
        received(from_front.at[1, :, 1], 2)
        received(from_back.at[1, pl.ds(0, side - 1)], 3)
        sig = spectrum(joined(1, 1), all_first, all_turns)
        back_out[...] = inverse(sig, gain, all_turns, all_last).reshape(back_out.shape)
        for d in same:
            remote(back_out.at[d], results.at[1, own], side + d, 3, 5).start()
        results[1, own] = back_out[own]
        received(results.at[0], 4)
        received(results.at[1, pl.ds(0, side - 1)], 5)
        finish()
        sent(sends.at[:, 0], 0)
        sent(sends.at[:, 1, pl.ds(0, side - 1)], 1)
        sent(back_out.at[pl.ds(0, side - 1)], 3)

    @pl.when(me < devices - 1)
    def _():
        halo_copy.wait_send()


def fused(tokens, norm_gain, w_in, short_filter, long_filter, medium_filter, skip_gain, w_out):
    rows, width = tokens.shape
    devices = lax.axis_size("seq")
    side = devices // 2
    chans = width // devices
    lanes, fine = rows // 2, chans // 2
    all_first, middle, all_last, *all_turns = tables(2 * devices, lanes, fine)
    front_first, _, front_last, *front_turns = tables(devices, lanes, chans)
    order = np.arange(width).reshape(side, 2, 2, fine).transpose(0, 2, 1, 3).reshape(-1)

    def split(matrix):
        return np.concatenate([matrix[:, :width], matrix[:, width:]], axis=0)

    matrices = [
        all_first,
        front_first[:, order],
        middle,
        split(front_last[order]),
        split(all_last[width // 2 :]),
    ]
    consts = [
        np.concatenate(matrices, axis=0),
        np.tile(np.concatenate([*all_turns, *front_turns], axis=0), (1, 2)),
    ]
    rim = 16
    held = [
        tokens,
        norm_gain.reshape(1, width),
        w_in,
        short_filter,
        long_filter,
        medium_filter,
        skip_gain.reshape(1, width),
        w_out,
        *[jnp.asarray(t) for t in consts],
    ]
    return pl.pallas_call(
        functools.partial(kernel, devices),
        out_shape=pltpu.VMEM((rows, width), bf16),
        in_specs=[pl.BlockSpec(memory_space=pl.ANY)] * len(held),
        out_specs=pl.BlockSpec(memory_space=pltpu.VMEM),
        scratch_shapes=[pltpu.VMEM(a.shape, a.dtype) for a in held]
        + [
            pltpu.VMEM((rim, width), bf16),
            pltpu.VMEM((rim + rows, 3 * width), f32),
            pltpu.VMEM((rows, width), f32),
            pltpu.VMEM((2, side, fine, rows), f32),
            pltpu.VMEM((2, 2, side, chans, rows), bf16),
            pltpu.VMEM((2, side, 2, chans, rows), bf16),
            pltpu.VMEM((2, side, chans, rows), bf16),
            pltpu.VMEM((side, 2, chans, rows), bf16),
            pltpu.VMEM((side, chans, rows), bf16),
            pltpu.VMEM((2, side, chans, rows), bf16),
            pltpu.SemaphoreType.REGULAR,
            pltpu.SemaphoreType.DMA((5,)),
            pltpu.SemaphoreType.DMA((2,)),
            pltpu.SemaphoreType.DMA((4,)),
            pltpu.SemaphoreType.DMA((6,)),
        ],
        compiler_params=pltpu.CompilerParams(collective_id=0, has_side_effects=True),
    )(*held)


def solution(mesh):
    placed = (P(("groups", "seq"), None), P(), P(), P(), P("seq", None), P(), P(), P())

    def step(tokens, norm_gain, w_in, short_filter, long_filter, medium_filter, skip_gain, w_out):
        chans = tokens.shape[1] // mesh.shape["seq"]
        whole_tiles = chans == 16 and tokens.shape[0] == tokens.shape[1]
        body = fused if whole_tiles else local
        return body(tokens, norm_gain, w_in, short_filter, long_filter, medium_filter, skip_gain, w_out)

    return jax.shard_map(
        step, mesh=mesh, in_specs=placed, out_specs=P(("groups", "seq"), None), check_vma=False
    )
```

```python
import functools
import math

import jax
import jax.numpy as jnp
import numpy as np
from jax import lax
from jax.experimental import pallas as pl
from jax.experimental.pallas import tpu as pltpu
from jax.sharding import PartitionSpec as P

epsilon = 1e-06
bf16 = jnp.bfloat16
f32 = jnp.float32


def tables(devices, tok_rows, chans):
    full = devices * tok_rows
    idx = np.arange(devices)
    angle = 2.0 * math.pi * ((idx[:, None] * (4 * idx[None, :] + 1)) % (4 * devices)) / (4 * devices)
    eye = np.eye(chans)
    outer_cos = np.kron(np.cos(angle), eye)
    outer_sin = np.kron(np.sin(angle), eye)
    first = np.concatenate([outer_cos.T, -outer_sin.T], axis=0)
    last = np.concatenate([outer_cos, -outer_sin], axis=1) / full
    pos = np.arange(tok_rows)
    turn = 2.0 * math.pi * ((4 * idx[:, None] + 1) * pos[None, :]) / (4 * full)
    tw_cos = np.repeat(np.cos(turn), chans, axis=0)
    tw_sin = np.repeat(np.sin(turn), chans, axis=0)
    inner = 2.0 * math.pi * (pos[:, None] * pos[None, :] % tok_rows) / tok_rows
    cos_t, sin_t = np.cos(inner), np.sin(inner)
    middle = np.block([[cos_t, -sin_t], [sin_t, cos_t]])
    return (
        first.astype(bf16),
        middle.astype(bf16),
        last.astype(bf16),
        tw_cos.astype(np.float32),
        tw_sin.astype(np.float32),
    )


def dot(a, b):
    return jnp.dot(a, b, preferred_element_type=f32)


def forward(rows, first, middle, tw_cos, tw_sin):
    half = rows.shape[0]
    part = dot(first, rows)
    re, im = part[:half], part[half:]
    turned = jnp.concatenate([re * tw_cos + im * tw_sin, im * tw_cos - re * tw_sin], axis=1)
    return dot(turned.astype(bf16), middle)


def convolve(sig, fil, first, middle, last, tw_cos, tw_sin):
    width = sig.shape[1]
    spec = forward(sig, first, middle, tw_cos, tw_sin)
    gain = forward(fil, first, middle, tw_cos, tw_sin)
    sr, si, gr, gi = spec[:, :width], spec[:, width:], gain[:, :width], gain[:, width:]
    prod = jnp.concatenate([sr * gi + si * gr, sr * gr - si * gi], axis=1).astype(bf16)
    back = dot(prod, middle)
    im, re = back[:, :width], back[:, width:]
    turned = jnp.concatenate([re * tw_cos - im * tw_sin, re * tw_sin + im * tw_cos], axis=0)
    return dot(last, turned.astype(bf16))


def from_behind(array, axis, by):
    devices = lax.axis_size(axis)
    pairs = [(i, i + by) for i in range(devices) if 0 <= i + by < devices]
    return lax.ppermute(array, axis, pairs)


def local(tokens, norm_gain, w_in, short_filter, long_filter, medium_filter, skip_gain, w_out):
    tok_rows, chan_width = tokens.shape
    devices = lax.axis_size("seq")
    my_index = lax.axis_index("seq")
    chans = chan_width // devices
    consts = [jnp.asarray(t) for t in tables(devices, tok_rows, chans)]
    med = jnp.pad(medium_filter, ((0, tok_rows - medium_filter.shape[0]), (0, 0)))
    med = med.at[0].add(skip_gain)
    taps = (long_filter + jnp.where(my_index == 0, med, 0.0)).astype(bf16)
    inputs = tokens.astype(f32)
    mean_sq = jnp.mean(inputs * inputs, axis=-1, keepdims=True)
    normed = (inputs * lax.rsqrt(mean_sq + epsilon) * norm_gain).astype(bf16)
    projected = dot(normed, w_in).astype(bf16)
    taps_count = short_filter.shape[0]
    rim_rows = from_behind(projected[tok_rows - (taps_count - 1) :], "seq", 1)
    extended = jnp.concatenate([rim_rows, projected], axis=0)
    short_mix = jnp.zeros((tok_rows, projected.shape[1]), f32)
    for tap_num in range(taps_count):
        begin = taps_count - 1 - tap_num
        short_mix = short_mix + short_filter[tap_num] * extended[begin : begin + tok_rows]
    query_part = short_mix[:, 0:chan_width]
    signal = short_mix[:, chan_width : 2 * chan_width] * short_mix[:, 2 * chan_width :]

    def spread(array):
        split = array.astype(bf16).T.reshape(devices, chans, tok_rows)
        return lax.all_to_all(split, "seq", 0, 0, tiled=True).reshape(chan_width, tok_rows)

    mixed = convolve(spread(signal), spread(taps), *consts)
    back = spread_back(mixed, devices, chans)
    mixed_out = (query_part * back.T.astype(f32)).astype(bf16)
    return dot(mixed_out, w_out).astype(bf16)


def spread_back(mixed, devices, chans):
    split = mixed.astype(bf16).reshape(devices, chans, mixed.shape[1])
    return lax.all_to_all(split, "seq", 0, 0, tiled=True).reshape(mixed.shape)


def rms_normed(rows, gain):
    rows = rows.astype(f32)
    mean_sq = jnp.mean(rows * rows, axis=-1, keepdims=True)
    return (rows * lax.rsqrt(mean_sq + epsilon) * gain).astype(bf16)


def relative(own, count):
    steps = []
    bit = 1
    while bit < count:
        steps.append((bit, bit * (1 - 2 * (own // bit % 2))))
        bit *= 2
    return [own + sum(step for bit, step in steps if off // bit % 2) for off in range(count - 1, -1, -1)]


def kernel(
    devices,
    tokens_hbm,
    gain_hbm,
    w_in_hbm,
    short_hbm,
    long_hbm,
    med_hbm,
    skip_hbm,
    w_out_hbm,
    matrices_hbm,
    turns_hbm,
    out_ref,
    tokens,
    gain_ref,
    w_in,
    short_ref,
    long_taps,
    med,
    skip_ref,
    w_out,
    matrices,
    turns,
    halo,
    extended,
    signal,
    later,
    sends,
    from_front,
    from_back,
    front_out,
    back_out,
    results,
    ready,
    local_sem,
    halo_sem,
    send_sem,
    recv_sem,
):
    me = lax.axis_index("seq")
    rows, width = tokens.shape
    side = devices // 2
    chans = width // devices
    half = width // 2
    lanes = rows // 2
    fine = chans // 2
    in_front = me < side
    own = lax.rem(me, side)
    cross = relative(own, side)
    same = cross[:-1]
    plane = side // 2
    near = relative(lax.rem(own, plane), plane)
    far = [plane + x for x in near]
    rim = halo.shape[0]
    def copies(pairs):
        return [
            pltpu.make_async_copy(source, target, local_sem.at[num])
            for num, (source, target) in enumerate(pairs)
        ]

    loads = copies(
        [
            (long_hbm, long_taps),
            (tokens_hbm, tokens),
            (gain_hbm, gain_ref),
            (w_in_hbm, w_in),
            (short_hbm, short_ref),
        ]
    )
    later_loads = copies([(matrices_hbm, matrices), (w_out_hbm, w_out), (turns_hbm, turns)])
    for load in loads[:5]:
        load.start()

    in_back = jnp.logical_not(in_front)
    barrier = pltpu.get_barrier_semaphore()

    def announce(semaphore, peer):
        pl.semaphore_signal(
            semaphore, inc=1, device_id={"seq": peer}, device_id_type=pl.DeviceIdType.MESH
        )

    @pl.when(in_front)
    def _():
        for d in same:
            announce(barrier, d)
        for d in cross:
            announce(barrier, side + d)

    @pl.when(in_back)
    def _():
        for d in same[-1:] + same[:-1]:
            announce(barrier, side + d)

    for load in loads[5:]:
        load.start()

    @pl.when(me == devices - 1)
    def _():
        pl.semaphore_wait(barrier, devices - 1)
        for d in cross:
            announce(ready, d)

    def remote(source, target, peer, sent, received):
        return pltpu.make_async_remote_copy(
            src_ref=source,
            dst_ref=target,
            send_sem=send_sem.at[sent],
            recv_sem=recv_sem.at[received],
            device_id={"seq": peer},
            device_id_type=pl.DeviceIdType.MESH,
        )

    def received(ref, num):
        remote(ref, ref, 0, num, num).wait_recv()

    def sent(ref, num):
        remote(ref, ref, 0, num, num).wait_send()

    def same_from_front(kind):
        for d in same:
            remote(sends.at[kind, :, d], from_front.at[kind, own], d, 0, 2 * kind).start()
        from_front[kind, own] = sends[kind, :, own]

    def cross_from_front(kind):
        for d in cross:
            target = from_front.at[kind, own, 1]
            remote(sends.at[kind, 1, d], target, side + d, 1, 2 * kind).start()

    def same_from_back(kind):
        for d in same:
            target = from_back.at[kind, own]
            remote(sends.at[kind, 1, d], target, side + d, 1, 2 * kind + 1).start()
        from_back[kind, own] = sends[kind, 1, own]

    def cross_from_back(kind):
        for d in cross:
            target = from_back.at[kind, own]
            remote(sends.at[kind, 0, d], target, d, 0, 2 * kind + 1).start()

    def project(part_normed, begin):
        return dot(part_normed, w_in[:, begin:]).astype(bf16).astype(f32)

    def mix(part, begin, count):
        cols = pl.ds(part * width, width)
        total = short_ref[0:1, cols] * extended[rim + begin : rim + begin + count, cols]
        for tap in range(1, short_ref.shape[0]):
            start = rim + begin - tap
            total = total + short_ref[tap : tap + 1, cols] * extended[start : start + count, cols]
        return total

    def turn(ref, begin):
        block = ref[begin : begin + lanes, :].T.reshape(2, side, 2, fine, lanes)
        return jnp.concatenate([block[:, :, 0], block[:, :, 1]], axis=3)

    halo_copy = pltpu.make_async_remote_copy(
        src_ref=tokens.at[pl.ds(rows - rim, rim)],
        dst_ref=halo,
        send_sem=halo_sem.at[0],
        recv_sem=halo_sem.at[1],
        device_id={"seq": lax.rem(me + 1, devices)},
        device_id_type=pl.DeviceIdType.MESH,
    )
    loads[0].wait()

    @pl.when(me == 0)
    def _():
        for load in copies([(med_hbm, med)]):
            load.start()
            load.wait()
        for load in copies([(skip_hbm, skip_ref)]):
            load.start()
            load.wait()
        long_taps[0 : med.shape[0], :] += med[...]
        long_taps[0:1, :] += skip_ref[...]

    sends[0] = jnp.concatenate([turn(long_taps, 0), turn(long_taps, lanes)], axis=2).astype(bf16)
    loads[1].wait()

    @pl.when(in_back)
    def _():
        @pl.when(me < devices - 1)
        def _():
            pl.semaphore_wait(barrier, devices - 1)
            halo_copy.start()

        cross_from_back(0)
        same_from_back(0)

    for load in loads[2:]:
        load.wait()
    for load in later_loads:
        load.start()
    normed = rms_normed(tokens[...], gain_ref[...])
    extended[rim:, width:] = project(normed, width)
    extended[0:rim, :] = jnp.zeros((rim, 3 * width), f32)
    signal[...] = mix(1, 0, rows) * mix(2, 0, rows)
    later[...] = turn(signal, lanes)

    @pl.when(in_front)
    def _():
        pl.semaphore_wait(barrier, side - 1)

        @pl.when(me < side - 1)
        def _():
            halo_copy.start()

        same_from_front(0)

    @pl.when(me > 0)
    def _():
        halo_copy.wait_recv()
        extended[0:rim, :] = project(rms_normed(halo[...], gain_ref[...]), 0)
        signal[0:rim, :] = mix(1, 0, rim) * mix(2, 0, rim)

    sends[1] = jnp.concatenate([turn(signal, 0), later[...]], axis=2).astype(bf16)

    @pl.when(in_front)
    def _():
        same_from_front(1)
        pl.semaphore_wait(ready, 1)

        @pl.when(me == side - 1)
        def _():
            halo_copy.start()

        cross_from_front(0)
        cross_from_front(1)

    @pl.when(in_back)
    def _():
        same_from_back(1)
        cross_from_back(1)

    extended[rim:, :width] = dot(normed, w_in[:, :width]).astype(bf16).astype(f32)
    query = mix(0, 0, rows).T
    for load in later_loads:
        load.wait()
    sizes = [2 * width, 2 * width, width, 2 * width, width]
    begins = [sum(sizes[:num]) for num in range(len(sizes))]
    views = [matrices.at[pl.ds(begin, size)] for begin, size in zip(begins, sizes)]
    all_first, front_first, middle, front_last, all_last = views
    all_turns, front_turns = (turns.at[pl.ds(side_begin, 2 * width)] for side_begin in (0, 2 * width))

    def stacked(left, right):
        pieces = [(left[:, :lanes], right[:, :lanes]), (left[:, lanes:], right[:, lanes:])]
        return jnp.concatenate([jnp.concatenate(pair, axis=1) for pair in pieces], axis=0)

    def spread(array):
        return jnp.concatenate([array[:width], array[width:]], axis=1)

    def spectrum(block, first, turns):
        part = dot(first[...], block)
        re, im = part[:width], part[width:]
        cos_t, sin_t = turns[:width], turns[width:]
        turned = stacked(re * cos_t + im * sin_t, im * cos_t - re * sin_t)
        spec = dot(turned.astype(bf16), middle[...])
        return spec[:, :lanes], spec[:, lanes:]

    def inverse(sig, gain, turns, last):
        (sr, si), (gr, gi) = sig, gain
        prod = jnp.concatenate([sr * gi + si * gr, sr * gr - si * gi], axis=1)
        back = dot(prod.astype(bf16), middle[...])
        im, re = spread(back[:, :lanes]), spread(back[:, lanes:])
        cos_t, sin_t = turns[:width], turns[width:]
        left, right = re * cos_t - im * sin_t, re * sin_t + im * cos_t
        count = last.shape[0] // 2
        total = dot(last[:count], left.astype(bf16)) + dot(last[count:], right.astype(bf16))
        return total.astype(bf16)

    def joined(kind, which):
        front = from_front[kind, :, which].reshape(half, rows)
        return jnp.concatenate([front, from_back[kind].reshape(half, rows)], axis=0)

    def finish():
        mixed = results[...].astype(f32)
        early, late = mixed[:, :, :fine], mixed[:, :, fine:]
        sides = [
            jnp.concatenate([early[:, :, :, cut], late[:, :, :, cut]], axis=3)
            for cut in (slice(0, lanes), slice(lanes, rows))
        ]
        mixed = jnp.concatenate(sides, axis=2).reshape(width, rows)
        gated = (query * mixed).astype(bf16).T
        out_ref[...] = dot(gated, w_out[...]).astype(bf16)

    @pl.when(in_front)
    def _():
        received(from_front.at[0, pl.ds(0, side - 1)], 0)
        gain = spectrum(from_front[0].reshape(width, rows), front_first, front_turns)
        received(from_front.at[1, pl.ds(0, side - 1)], 2)
        sig = spectrum(from_front[1].reshape(width, rows), front_first, front_turns)
        front_out[...] = inverse(sig, gain, front_turns, front_last).reshape(front_out.shape)
        for d in same:
            remote(front_out.at[d], results.at[:, own], d, 2, 4).start()
        results[:, own] = front_out[own]
        received(from_back.at[0], 1)
        back_gain = spectrum(joined(0, 0), all_first, all_turns)
        received(from_back.at[1], 3)
        sig = spectrum(joined(1, 0), all_first, all_turns)
        back_out[...] = inverse(sig, back_gain, all_turns, all_last).reshape(back_out.shape)
        for d in [0, 1, 4, 5, 2, 3, 6, 7]:
            remote(back_out.at[d], results.at[0, own], side + d, 3, 4).start()
        received(results.at[:, pl.ds(0, side - 1)], 4)
        finish()
        sent(sends.at[:, :, pl.ds(0, side - 1)], 0)
        sent(sends.at[:, 1], 1)
        sent(front_out.at[pl.ds(0, side - 1)], 2)
        sent(back_out, 3)

    @pl.when(jnp.logical_not(in_front))
    def _():
        received(from_front.at[0, :, 1], 0)
        received(from_back.at[0, pl.ds(0, side - 1)], 1)
        gain = spectrum(joined(0, 1), all_first, all_turns)
        received(from_front.at[1, :, 1], 2)
        received(from_back.at[1, pl.ds(0, side - 1)], 3)
        sig = spectrum(joined(1, 1), all_first, all_turns)
        back_out[...] = inverse(sig, gain, all_turns, all_last).reshape(back_out.shape)
        for d in same:
            remote(back_out.at[d], results.at[1, own], side + d, 3, 5).start()
        results[1, own] = back_out[own]
        received(results.at[0], 4)
        received(results.at[1, pl.ds(0, side - 1)], 5)
        finish()
        sent(sends.at[:, 0], 0)
        sent(sends.at[:, 1, pl.ds(0, side - 1)], 1)
        sent(back_out.at[pl.ds(0, side - 1)], 3)

    @pl.when(me < devices - 1)
    def _():
        halo_copy.wait_send()


def fused(tokens, norm_gain, w_in, short_filter, long_filter, medium_filter, skip_gain, w_out):
    rows, width = tokens.shape
    devices = lax.axis_size("seq")
    side = devices // 2
    chans = width // devices
    lanes, fine = rows // 2, chans // 2
    all_first, middle, all_last, *all_turns = tables(2 * devices, lanes, fine)
    front_first, _, front_last, *front_turns = tables(devices, lanes, chans)
    order = np.arange(width).reshape(side, 2, 2, fine).transpose(0, 2, 1, 3).reshape(-1)

    def split(matrix):
        return np.concatenate([matrix[:, :width], matrix[:, width:]], axis=0)

    matrices = [
        all_first,
        front_first[:, order],
        middle,
        split(front_last[order]),
        split(all_last[width // 2 :]),
    ]
    consts = [
        np.concatenate(matrices, axis=0),
        np.tile(np.concatenate([*all_turns, *front_turns], axis=0), (1, 2)),
    ]
    rim = 16
    held = [
        tokens,
        norm_gain.reshape(1, width),
        w_in,
        short_filter,
        long_filter,
        medium_filter,
        skip_gain.reshape(1, width),
        w_out,
        *[jnp.asarray(t) for t in consts],
    ]
    return pl.pallas_call(
        functools.partial(kernel, devices),
        out_shape=pltpu.VMEM((rows, width), bf16),
        in_specs=[pl.BlockSpec(memory_space=pl.ANY)] * len(held),
        out_specs=pl.BlockSpec(memory_space=pltpu.VMEM),
        scratch_shapes=[pltpu.VMEM(a.shape, a.dtype) for a in held]
        + [
            pltpu.VMEM((rim, width), bf16),
            pltpu.VMEM((rim + rows, 3 * width), f32),
            pltpu.VMEM((rows, width), f32),
            pltpu.VMEM((2, side, fine, rows), f32),
            pltpu.VMEM((2, 2, side, chans, rows), bf16),
            pltpu.VMEM((2, side, 2, chans, rows), bf16),
            pltpu.VMEM((2, side, chans, rows), bf16),
            pltpu.VMEM((side, 2, chans, rows), bf16),
            pltpu.VMEM((side, chans, rows), bf16),
            pltpu.VMEM((2, side, chans, rows), bf16),
            pltpu.SemaphoreType.REGULAR,
            pltpu.SemaphoreType.DMA((5,)),
            pltpu.SemaphoreType.DMA((2,)),
            pltpu.SemaphoreType.DMA((4,)),
            pltpu.SemaphoreType.DMA((6,)),
        ],
        compiler_params=pltpu.CompilerParams(collective_id=0, has_side_effects=True),
    )(*held)


def solution(mesh):
    placed = (P(("groups", "seq"), None), P(), P(), P(), P("seq", None), P(), P(), P())

    def step(tokens, norm_gain, w_in, short_filter, long_filter, medium_filter, skip_gain, w_out):
        chans = tokens.shape[1] // mesh.shape["seq"]
        whole_tiles = chans == 16 and tokens.shape[0] == tokens.shape[1]
        body = fused if whole_tiles else local
        return body(tokens, norm_gain, w_in, short_filter, long_filter, medium_filter, skip_gain, w_out)

    return jax.shard_map(
        step, mesh=mesh, in_specs=placed, out_specs=P(("groups", "seq"), None), check_vma=False
    )
```
